128 devices in a mesh: ctx: 32 (over x, z, core), wsh: 4 (over y).
Axes of the slice: x: 4, y: 4, z: 4, core: 2. Of those that a mesh axis runs over, the one named last changes fastest.
Arguments:
- tokens: bfloat16 [4, 4096, 768], P('wsh', 'ctx'), may hold values from -6 to 6
- cotangent: bfloat16 [4, 4096, 768], P('wsh', 'ctx'), may hold values from -6 to 6
- pair_of_device: int32 [32], replicated, may hold values from 0 to 31, each once
- qkv_weight: float32 [1, 768, 2304], P(None, ('ctx', 'wsh')), may hold values from -0.3125 to 0.3125
- out_weight: float32 [1, 768, 768], P(None, ('ctx', 'wsh')), may hold values from -1 to 1
- fc1_weight: float32 [1, 768, 3072], P(None, ('ctx', 'wsh')), may hold values from -0.21875 to 0.21875
- fc2_weight: float32 [1, 768, 3072], P(None, ('ctx', 'wsh')), may hold values from -0.109375 to 0.109375
- vectors: float32 [1, 12, 768], replicated, may hold values from -2.5 to 2.5, as said below
- qkv_moment: float32 [1, 768, 2304], P(None, ('ctx', 'wsh')), may hold values from -80 to 80
- qkv_second: float32 [1, 768, 2304], P(None, ('ctx', 'wsh')), may hold values from 8.192 to 131.072
- out_moment: float32 [1, 768, 768], P(None, ('ctx', 'wsh')), may hold values from -32 to 32
- out_second: float32 [1, 768, 768], P(None, ('ctx', 'wsh')), may hold values from 1.31072 to 21.2992
- fc1_moment: float32 [1, 768, 3072], P(None, ('ctx', 'wsh')), may hold values from -40 to 40
- fc1_second: float32 [1, 768, 3072], P(None, ('ctx', 'wsh')), may hold values from 2.048 to 32.768
- fc2_moment: float32 [1, 768, 3072], P(None, ('ctx', 'wsh')), may hold values from -80 to 80
- fc2_second: float32 [1, 768, 3072], P(None, ('ctx', 'wsh')), may hold values from 6.5536 to 106.496
- vector_moment: float32 [1, 12, 768], replicated, may hold values from -80 to 80
- vector_second: float32 [1, 12, 768], replicated, may hold values from 8.192 to 131.072
Outputs:
- block_out: float32 [4, 4096, 768], P('wsh', 'ctx')
- input_grad: float32 [4, 4096, 768], P('wsh', 'ctx')
- qkv_moment_new: float32 [1, 768, 2304], P(None, ('ctx', 'wsh'))
- qkv_second_new: float32 [1, 768, 2304], P(None, ('ctx', 'wsh'))
- qkv_weight_new: float32 [1, 768, 2304], P(None, ('ctx', 'wsh'))
- out_moment_new: float32 [1, 768, 768], P(None, ('ctx', 'wsh'))
- out_second_new: float32 [1, 768, 768], P(None, ('ctx', 'wsh'))
- out_weight_new: float32 [1, 768, 768], P(None, ('ctx', 'wsh'))
- fc1_moment_new: float32 [1, 768, 3072], P(None, ('ctx', 'wsh'))
- fc1_second_new: float32 [1, 768, 3072], P(None, ('ctx', 'wsh'))
- fc1_weight_new: float32 [1, 768, 3072], P(None, ('ctx', 'wsh'))
- fc2_moment_new: float32 [1, 768, 3072], P(None, ('ctx', 'wsh'))
- fc2_second_new: float32 [1, 768, 3072], P(None, ('ctx', 'wsh'))
- fc2_weight_new: float32 [1, 768, 3072], P(None, ('ctx', 'wsh'))
- vector_moment_new: float32 [1, 12, 768], replicated
- vector_second_new: float32 [1, 12, 768], replicated
- vector_new: float32 [1, 12, 768], replicated
The draws below stay inside these ranges and needn't reach their ends.
Inputs may be any that keep to these rules, and one draw needn't show every extreme that they name: `pair_of_device`: each pair number appears once. `vectors`: rows 0 and 5 of each layer are positive.
All inputs are finite; a program needn't handle non-finite values.
Results may differ from the reference program's by a relative error of at most 0.017.
The reference program's roundings to bfloat16 on the way count: a program that leaves them out, or rounds other values in their place, can miss the bound.
Values may be sent and summed in bfloat16 or wider, within the bound.
No kernel may reach another device: no remote copies, remote signals or barrier semaphores. Data moves between devices by JAX's collectives and lax.ppermute only.
A program may use at most 192 MiB of HBM per device.

```python
import math
import jax
import jax.numpy as jnp
from jax import lax

D = 768
HEADS = 12
HD = 64
FF = 3072
LAYERS = 1
STEP = 5
BLK = 64
SEQS = 4
SEQ_LEN = 4096
N_CTX = 32


def draw_vectors(key, part):
    key = jax.random.fold_in(key, 7)
    key_gain, key_bias = jax.random.split(key)
    shape = (LAYERS, 12, D)
    gains = jnp.exp(jax.random.uniform(key_gain, shape, jnp.float32, -0.7, 0.7))
    biases = jnp.clip(jax.random.normal(key_bias, shape, jnp.float32) * 0.5, -2.5, 2.5)
    row_number = jnp.arange(12, dtype=jnp.int32)[None, :, None]
    is_gain = (row_number == 0) | (row_number == 5)
    return jnp.where(is_gain, gains, biases)


def level_of(rng, dims, shards, low, high):
    factor_of, own = 1.0, jax.random.fold_in(rng, 6)
    for dim, blocks in shards:
        draws = jnp.exp(jax.random.uniform(jax.random.fold_in(own, dim), (blocks,), jnp.float32, low / len(shards), high / len(shards)))
        factor_of = factor_of * jnp.repeat(draws, dims[dim] // blocks).reshape([-1 if axis == dim else 1 for axis in range(len(dims))])
    return factor_of


def noise(key, extent, scale, most, cuts=(), kind=jnp.bfloat16):
    values = scale * jax.random.normal(key, extent, jnp.float32)
    if cuts:
        values = values * level_of(key, extent, cuts, -0.22, 0.18)
    return jnp.clip(values, -most, most).astype(kind)


def setup_inputs(seed: int = 0) -> dict:
    key_of = jax.random.split(jax.random.key(seed), 19)
    tokens = noise(key_of[0], (SEQS, SEQ_LEN, D), 1.0, 6.0, ((0, 4), (1, 32)))
    cotangent = noise(key_of[1], (SEQS, SEQ_LEN, D), 1.0, 6.0, ((0, 4), (1, 32)))
    pair_of_device = jax.random.permutation(key_of[2], SEQ_LEN // (2 * BLK)).astype(jnp.int32)
    qkv_weight = noise(key_of[3], (LAYERS, D, 3 * D), (D // 2) ** -0.5, 0.3125, ((1, 128),), jnp.float32)
    out_weight = noise(key_of[4], (LAYERS, D, D), (max(8, D * 200 // SEQ_LEN)) ** -0.5, 1.0, ((1, 128),), jnp.float32)
    fc1_weight = noise(key_of[5], (LAYERS, D, FF), D ** -0.5, 0.21875, ((1, 128),), jnp.float32)
    fc2_weight = noise(key_of[6], (LAYERS, D, FF), FF ** -0.5, 0.109375, ((1, 128),), jnp.float32)
    vectors = draw_vectors(jax.random.fold_in(key_of[18], 71), 0)
    qkv_moment = noise(key_of[8], (LAYERS, D, 3 * D), (0.11 * (SEQS * SEQ_LEN) ** 0.5), 80.0, ((1, 128),), jnp.float32)
    qkv_second = jnp.clip(jnp.exp(math.log(131.072) - 2.7725887 * jax.random.uniform(key_of[9], (LAYERS, D, 3 * D), jnp.float32) ** level_of(key_of[9], (LAYERS, D, 3 * D), ((1, 128),), -0.2, 0.2)), 8.192, 131.072)
    out_moment = noise(key_of[10], (LAYERS, D, D), (0.044 * (SEQS * SEQ_LEN) ** 0.5), 32.0, ((1, 128),), jnp.float32)
    out_second = jnp.clip(jnp.exp(math.log(21.2992) - 2.7880929 * jax.random.uniform(key_of[11], (LAYERS, D, D), jnp.float32) ** level_of(key_of[11], (LAYERS, D, D), ((1, 128),), -0.2, 0.2)), 1.31072, 21.2992)
    fc1_moment = noise(key_of[12], (LAYERS, D, FF), (0.055 * (SEQS * SEQ_LEN) ** 0.5), 40.0, ((1, 128),), jnp.float32)
    fc1_second = jnp.clip(jnp.exp(math.log(32.768) - 2.7725887 * jax.random.uniform(key_of[13], (LAYERS, D, FF), jnp.float32) ** level_of(key_of[13], (LAYERS, D, FF), ((1, 128),), -0.2, 0.2)), 2.048, 32.768)
    fc2_moment = noise(key_of[14], (LAYERS, D, FF), (0.1 * (SEQS * SEQ_LEN) ** 0.5), 80.0, ((1, 128),), jnp.float32)
    fc2_second = jnp.clip(jnp.exp(math.log(106.496) - 2.78809295 * jax.random.uniform(key_of[15], (LAYERS, D, FF), jnp.float32) ** level_of(key_of[15], (LAYERS, D, FF), ((1, 128),), -0.2, 0.2)), 6.5536, 106.496)
    vector_moment = noise(key_of[16], (LAYERS, 12, D), (0.11 * (SEQS * SEQ_LEN) ** 0.5), 80.0, (), jnp.float32)
    vector_second = jnp.clip(jnp.exp(jax.random.uniform(key_of[17], (LAYERS, 12, D), jnp.float32, math.log(8.192), math.log(131.072))), 8.192, 131.072)
    return {"tokens": tokens, "cotangent": cotangent, "pair_of_device": pair_of_device, "qkv_weight": qkv_weight, "out_weight": out_weight, "fc1_weight": fc1_weight, "fc2_weight": fc2_weight, "vectors": vectors, "qkv_moment": qkv_moment, "qkv_second": qkv_second, "out_moment": out_moment, "out_second": out_second, "fc1_moment": fc1_moment, "fc1_second": fc1_second, "fc2_moment": fc2_moment, "fc2_second": fc2_second, "vector_moment": vector_moment, "vector_second": vector_second}


@jax.custom_vjp
def low(v):
    return lax.optimization_barrier(v.astype(jnp.bfloat16)).astype(jnp.float32)

@jax.custom_vjp
def low_back(v):
    return v

def low_keep(v):
    return (low(v), None)

def low_pass(kept, grad):
    return (grad,)

def back_keep(v):
    return (v, None)

def back_low(kept, grad):
    return (low(grad),)
low.defvjp(low_keep, low_pass)
low_back.defvjp(back_keep, back_low)
EPS_NORM = 1e-05
NEGATIVE = -1e+30
BETA_ONE = 0.9
BETA_TWO = 0.999
RATE_MATRIX = 0.1
RATE_VECTOR = 0.5
DECAY_MATRIX = 0.1
EPS_ADAM = 1e-08
HIGHEST = lax.Precision.HIGHEST

def both_ways(value):
    return low(low_back(value))

def product(left, right):
    return jnp.dot(left, right, precision=HIGHEST)

def layer_norm(hidden, norm_gain, norm_shift):
    center = hidden - lax.optimization_barrier(jnp.mean(hidden, axis=-1, keepdims=True))
    spread = lax.optimization_barrier(jnp.mean(center * center, axis=-1, keepdims=True))
    return center * lax.rsqrt(spread + EPS_NORM) * norm_gain + norm_shift

def positions(pair_of_device):
    row_index = jnp.arange(SEQ_LEN, dtype=jnp.int32)
    device = row_index // (2 * BLK)
    within = row_index % (2 * BLK)
    pair_num = pair_of_device[device].astype(jnp.int32)
    block_num = jnp.where(within < BLK, pair_num, 2 * N_CTX - 1 - pair_num)
    return (block_num * BLK + within % BLK).astype(jnp.int32)

def attend(queries, key_rows, value_rows, places):
    block_size = min(512, SEQ_LEN)
    block_count = SEQ_LEN // block_size
    key_heads = key_rows.reshape(SEQ_LEN, HEADS, HD)
    value_heads = value_rows.reshape(SEQ_LEN, HEADS, HD)

    def one_block(element):
        query_block, place_block = element
        scores = jnp.einsum('qhd,khd->hqk', query_block, key_heads, precision=HIGHEST) * HD ** (-0.5)
        scores = low_back(scores)
        allowed = places[None, None, :] <= place_block[None, :, None]
        scores = jnp.where(allowed, scores, NEGATIVE)
        peak_row = lax.optimization_barrier(jnp.max(scores, axis=-1, keepdims=True))
        log_total = peak_row + jnp.log(lax.optimization_barrier(jnp.sum(jnp.exp(scores - peak_row), axis=-1, keepdims=True)))
        probs = low(jnp.exp(scores - log_total))
        return jnp.einsum('hqk,khd->qhd', probs, value_heads, precision=HIGHEST)
    outputs = lax.map(jax.checkpoint(one_block), (queries.reshape(block_count, block_size, HEADS, HD), places.reshape(block_count, block_size)))
    return outputs.reshape(SEQ_LEN, D)

def forward_pass(params, hidden, places):
    qkv_weight, out_weight, fc1_weight, fc2_weight, vectors = params
    for layer_at in range(LAYERS):
        vector = vectors[layer_at]
        normed = low(layer_norm(hidden, vector[0], vector[1]))
        projected = product(normed, low(qkv_weight[layer_at]))
        queries = both_ways(projected[:, :D] + vector[2])
        key_rows = both_ways(projected[:, D:2 * D])
        value_rows = both_ways(projected[:, 2 * D:] + vector[3])
        attended = both_ways(attend(queries, key_rows, value_rows, places))
        middle = hidden + low_back(product(attended, low(out_weight[layer_at])) + vector[4])
        normed_two = low(layer_norm(middle, vector[5], vector[6]))
        pre_active = low_back(product(normed_two, low(fc1_weight[layer_at])) + vector[8:12].reshape(FF))
        active = low(jax.nn.gelu(pre_active))
        hidden = middle + low_back(product(active, low(fc2_weight[layer_at]).T) + vector[7])
    return hidden

def adamw(weight, moment, second, gradient, step_rate, decay_rate):
    moment_new = BETA_ONE * moment + (1.0 - BETA_ONE) * gradient
    second_new = BETA_TWO * second + (1.0 - BETA_TWO) * gradient * gradient
    moment_hat = moment_new / (1.0 - BETA_ONE ** STEP)
    second_hat = second_new / (1.0 - BETA_TWO ** STEP)
    weight_new = weight - step_rate * (moment_hat / (jnp.sqrt(second_hat) + EPS_ADAM) + decay_rate * weight)
    return (moment_new, second_new, weight_new)

def reference(tokens, cotangent, pair_of_device, qkv_weight, out_weight, fc1_weight, fc2_weight, vectors, qkv_moment, qkv_second, out_moment, out_second, fc1_moment, fc1_second, fc2_moment, fc2_second, vector_moment, vector_second):
    places = positions(pair_of_device)
    params = (qkv_weight, out_weight, fc1_weight, fc2_weight, vectors)

    def per_sequence(totals, element):
        inputs, tangent = element

        def forward(weights, hidden):
            return forward_pass(weights, hidden, places)
        result, pullback = jax.vjp(forward, params, inputs.astype(jnp.float32))
        weight_grads, input_grad = pullback(tangent.astype(jnp.float32))
        totals = jax.tree.map(jnp.add, totals, weight_grads)
        return (totals, (result, input_grad))
    zero_tree = jax.tree.map(jnp.zeros_like, params)
    totals, (block_out, input_grad) = lax.scan(per_sequence, zero_tree, (tokens, cotangent))
    qkv_new = adamw(qkv_weight, qkv_moment, qkv_second, totals[0], RATE_MATRIX, DECAY_MATRIX)
    out_new = adamw(out_weight, out_moment, out_second, totals[1], RATE_MATRIX, DECAY_MATRIX)
    fc1_new = adamw(fc1_weight, fc1_moment, fc1_second, totals[2], RATE_MATRIX, DECAY_MATRIX)
    fc2_new = adamw(fc2_weight, fc2_moment, fc2_second, totals[3], RATE_MATRIX, DECAY_MATRIX)
    vec_new = adamw(vectors, vector_moment, vector_second, totals[4], RATE_VECTOR, 0.0)
    return (block_out, input_grad, qkv_new[0], qkv_new[1], qkv_new[2], out_new[0], out_new[1], out_new[2], fc1_new[0], fc1_new[1], fc1_new[2], fc2_new[0], fc2_new[1], fc2_new[2], vec_new[0], vec_new[1], vec_new[2])
```

```python
import jax
import jax.numpy as jnp
import numpy as np
from jax import lax
from jax.experimental import pallas as pl
from jax.experimental.pallas import tpu as pltpu
from jax.sharding import Mesh
from jax.sharding import PartitionSpec as P

D = 768
HEADS = 12
HD = 64
FF = 3072
LAYERS = 1
STEP = 5

EPS_NORM = 1e-05
NEGATIVE = -1e30
BETA_ONE = 0.9
BETA_TWO = 0.999
RATE_MATRIX = 0.1
RATE_VECTOR = 0.5
DECAY_MATRIX = 0.1
EPS_ADAM = 1e-08

NX = 4
NZ = 4
NC = 2
NY = 4
GH = HEADS // NX
GD = GH * HD
ROWS = 128
BLK = 64
QROWS = NX * ROWS
SEQ = 4096
NBLK = SEQ // BLK
CHUNK = 1024
GB = 4
WAYS = BLK * GB
BF = jnp.bfloat16
F32 = jnp.float32
VMEM = pltpu.VMEM
SMEM = pltpu.SMEM


def layer_norm(hidden, norm_gain, norm_shift):
    center = hidden - jnp.mean(hidden, axis=-1, keepdims=True)
    spread = jnp.mean(center * center, axis=-1, keepdims=True)
    return center * lax.rsqrt(spread + EPS_NORM) * norm_gain + norm_shift


def adamw(weight, moment, second, gradient, step_rate, decay_rate):
    moment_new = BETA_ONE * moment + (1.0 - BETA_ONE) * gradient
    second_new = BETA_TWO * second + (1.0 - BETA_TWO) * gradient * gradient
    moment_hat = moment_new / (1.0 - BETA_ONE**STEP)
    second_hat = second_new / (1.0 - BETA_TWO**STEP)
    weight_new = weight - step_rate * (
        moment_hat / (jnp.sqrt(second_hat) + EPS_ADAM) + decay_rate * weight
    )
    return (moment_new, second_new, weight_new)


RIGHT = [(i, (i + 1) % 4) for i in range(4)]
LEFT = [(i, (i + 3) % 4) for i in range(4)]
SWAP = [(0, 1), (1, 0)]
EVEN = [(0, 1), (1, 0), (2, 3), (3, 2)]
ODD = [(1, 2), (2, 1), (3, 0), (0, 3)]


def ring_gather(part, axis):
    half = part.shape[0] // 2
    before = lax.ppermute(part, axis, RIGHT)
    after = lax.ppermute(part, axis, LEFT)
    far_low = lax.ppermute(before[:half], axis, RIGHT)
    far_high = lax.ppermute(after[half:], axis, LEFT)
    return jnp.concatenate([part, before, after, far_low, far_high], axis=0)


def ordered(gathered, axis):
    rows = gathered.shape[0] // 4
    me = lax.axis_index(axis)
    relative = lax.rem(4 + jnp.arange(4) - me, 4)
    slot = jnp.where(relative == 1, 2, jnp.where(relative == 2, 3, jnp.where(relative == 3, 1, 0)))
    return jnp.take(gathered.reshape(4, rows, -1), slot, axis=0).reshape(gathered.shape)


def gather_zc(part):
    own = ring_gather(part, "z")
    return own, lax.ppermute(own, "c", SWAP)


def copy_gather(part, axes):
    count = lax.axis_size(axes)
    return lax.all_to_all(jnp.broadcast_to(part[None], (count,) + part.shape), axes, 0, 0, tiled=True)


def widening():
    pick = np.zeros((D, 8 * 128), np.float32)
    feature = np.arange(D)
    pick[feature, feature // 6 * 8 + feature % 6] = 1.0
    return pick


def filling(part):
    pick = np.zeros((D, 8 * 128), np.float32)
    device = np.arange(128)
    pick[6 * device + part, 8 * device + 6] = 1.0
    pick[6 * device + 3 + part, 8 * device + 7] = 1.0
    return pick


def dot_nt(left, right):
    return lax.dot_general(left, right, (((1,), (1,)), ((), ())), preferred_element_type=F32)


def dot_nn(left, right):
    return lax.dot_general(left, right, (((1,), (0,)), ((), ())), preferred_element_type=F32)


def group_rows(ref, blocks, columns):
    return jnp.concatenate(
        [ref[pl.ds(pl.multiple_of(block * BLK, BLK), BLK), columns] for block in blocks], axis=0
    )


def store_group(ref, blocks, columns, value):
    for at, block in enumerate(blocks):
        rows = slice(at * BLK, (at + 1) * BLK)
        ref[pl.ds(pl.multiple_of(block * BLK, BLK), BLK), columns] = value[rows]


def group_places(blocks, shape, axis):
    index = lax.broadcasted_iota(jnp.int32, shape, axis)
    places = blocks[0] * BLK + index
    for at in range(1, len(blocks)):
        places = jnp.where(index < at * BLK, places, (blocks[at] - at) * BLK + index)
    return places


def group_of(tab, g):
    own = [tab[NBLK + GB * g + j] for j in range(GB)]
    return own, [tab[NBLK + 8 + GB * g + j] for j in range(GB)]


def sort_blocks(tab, sources, store, at=0):
    for source in sources:
        count = source.shape[0] // BLK

        def move(block, carry, source=source, at=at):
            place = tab[at + block]
            rows = source[pl.ds(pl.multiple_of(block * BLK, BLK), BLK), :]
            store(pl.multiple_of(place * BLK, BLK), rows)
            return carry

        lax.fori_loop(0, count, move, 0)
        at = at + count


def head_columns(head, part=0):
    return slice(part * GD + head * HD, part * GD + (head + 1) * HD)


def forward_kernel(tab, q, kv_own, kv_other, att, exact, stats, k_s, v_s):
    def store(at, rows):
        ones = jnp.ones((BLK, HD), BF)
        for head in range(GH):
            k_s[head, pl.ds(at, BLK), :] = rows[:, head_columns(head)]
            v_s[head, pl.ds(at, BLK), :] = jnp.concatenate(
                [rows[:, head_columns(head, 1)], ones], axis=1
            )

    sort_blocks(tab, (kv_own, kv_other), store)
    lane = lax.broadcasted_iota(jnp.int32, (WAYS, 128), 1)

    def group(g, carry):
        own, at_places = group_of(tab, g)
        places = group_places(at_places, (WAYS, 1), 0)
        queries = [
            group_rows(q, own, head_columns(h)) * jnp.asarray(0.125, BF)
            for h in range(GH)
        ]

        def chunk(at, state):
            start = pl.multiple_of(at * CHUNK, CHUNK)
            keys_at = start + lax.broadcasted_iota(jnp.int32, (WAYS, CHUNK), 1)
            allowed = keys_at <= places
            out = []
            for h in range(GH):
                peak, plain, extra = state[h]
                scores = dot_nt(queries[h], k_s[h, pl.ds(start, CHUNK), :])
                scores = jnp.where(allowed, scores, NEGATIVE)
                peak_new = jnp.maximum(peak, jnp.max(scores, axis=1, keepdims=True))
                shrink = jnp.exp(peak - peak_new)
                expo = jnp.exp(scores - peak_new)
                probs = expo.astype(BF)
                residue = (expo - probs.astype(F32)).astype(BF)
                values = v_s[h, pl.ds(start, CHUNK), :]
                plain = plain * shrink + dot_nn(probs, values)
                extra = extra * shrink + dot_nn(residue, values)
                out.append((peak_new, plain, extra))
            return tuple(out)

        zero = jnp.zeros((WAYS, 128), F32)
        begin = tuple((jnp.full((WAYS, 1), NEGATIVE, F32), zero, zero) for _ in range(GH))
        state = lax.fori_loop(0, lax.div(at_places[-1], CHUNK // BLK) + 1, chunk, begin)
        table = jnp.zeros((WAYS, 128), F32)
        for h in range(GH):
            peak, plain, extra = state[h]
            both = plain + extra
            mass = both[:, HD : HD + 1]
            store_group(att, own, head_columns(h), (plain[:, :HD] / mass).astype(BF))
            store_group(exact, own, head_columns(h), both[:, :HD] / mass)
            table = jnp.where(lane == h, peak + jnp.log(mass), table)
        store_group(stats, own, slice(0, 128), table)
        return carry

    lax.fori_loop(0, 8 // GB, group, 0)


def pack_kernel(back, exact, stats_in, packed, stats):
    lane = lax.broadcasted_iota(jnp.int32, (QROWS, 128), 1)
    table = stats_in[...]
    extra = jnp.zeros((QROWS, 128), F32)
    for h in range(GH):
        columns = head_columns(h)
        dot = jnp.sum(back[:, columns].astype(F32) * exact[:, columns], axis=1, keepdims=True)
        table = jnp.where(lane == GH + h, dot, table)
    stats[...] = table
    for j in range(2 * GH):
        value = table[:, j : j + 1]
        for t in range(3):
            piece = value.astype(BF).astype(F32)
            value = value - piece
            extra = jnp.where(lane == 3 * j + t, piece, extra)
    packed[:, :GD] = back[...]
    packed[:, GD:] = extra[:, : 256 - GD].astype(BF)


def query_kernel(tab, q, back, stats, kv_own, kv_other, grad, k_s, v_s):
    def store(at, rows):
        for head in range(GH):
            k_s[head, pl.ds(at, BLK), :] = rows[:, head_columns(head)]
            v_s[head, pl.ds(at, BLK), :] = rows[:, head_columns(head, 1)]

    sort_blocks(tab, (kv_own, kv_other), store)

    def group(g, carry):
        own, at_places = group_of(tab, g)
        places = group_places(at_places, (WAYS, 1), 0)
        table = group_rows(stats, own, slice(0, 128))
        queries = [
            group_rows(q, own, head_columns(h)) * jnp.asarray(0.125, BF)
            for h in range(GH)
        ]
        backs = [group_rows(back, own, head_columns(h)) for h in range(GH)]

        def chunk(at, state):
            start = pl.multiple_of(at * CHUNK, CHUNK)
            keys_at = start + lax.broadcasted_iota(jnp.int32, (WAYS, CHUNK), 1)
            allowed = keys_at <= places
            out = []
            for h in range(GH):
                keys = k_s[h, pl.ds(start, CHUNK), :]
                scores = dot_nt(queries[h], keys) - table[:, h : h + 1]
                expo = jnp.exp(jnp.where(allowed, scores, NEGATIVE))
                dots = dot_nt(backs[h], v_s[h, pl.ds(start, CHUNK), :])
                slopes = (expo * (dots - table[:, GH + h : GH + h + 1])).astype(BF)
                out.append(state[h] + dot_nn(slopes, keys))
            return tuple(out)

        begin = tuple(jnp.zeros((WAYS, HD), F32) for _ in range(GH))
        state = lax.fori_loop(0, lax.div(at_places[-1], CHUNK // BLK) + 1, chunk, begin)
        for h in range(GH):
            store_group(grad, own, head_columns(h), (state[h] * 0.125).astype(BF))
        return carry

    lax.fori_loop(0, 8 // GB, group, 0)


def key_kernel(tab, kv, q_all, x_all, pick, grad, q_s, d_s, r_s, row_s):
    def store_q(at, rows):
        for head in range(GH):
            q_s[head, pl.ds(at, BLK), :] = rows[:, head_columns(head)] * jnp.asarray(0.125, BF)

    def store_x(at, rows):
        for head in range(GH):
            d_s[head, pl.ds(at, BLK), :] = rows[:, head_columns(head)]
        r_s[pl.ds(at, BLK), :] = rows[:, 128:256]

    sort_blocks(tab, (q_all,), store_q, NBLK + 16)
    sort_blocks(tab, (x_all,), store_x, NBLK + 16)

    def rows_of(at, carry):
        start = pl.multiple_of(at * CHUNK, CHUNK)
        row_s[at] = dot_nt(pick[...], r_s[pl.ds(start, CHUNK), :])
        return carry

    lax.fori_loop(0, SEQ // CHUNK, rows_of, 0)

    def group(g, carry):
        own, at_places = group_of(tab, g)
        places = group_places(at_places, (WAYS, 1), 0)
        keys = [group_rows(kv, own, head_columns(h)) for h in range(GH)]
        values = [group_rows(kv, own, head_columns(h, 1)) for h in range(GH)]

        def chunk(at, state):
            start = pl.multiple_of(at * CHUNK, CHUNK)
            queries_at = start + lax.broadcasted_iota(jnp.int32, (WAYS, CHUNK), 1)
            allowed = places <= queries_at
            rows = row_s[at]
            out = []
            for h in range(GH):
                queries = q_s[h, pl.ds(start, CHUNK), :]
                backs = d_s[h, pl.ds(start, CHUNK), :]
                scores = dot_nt(keys[h], queries) - rows[h : h + 1, :]
                expo = jnp.exp(jnp.where(allowed, scores, NEGATIVE))
                dots = dot_nt(values[h], backs)
                slopes = (expo * (dots - rows[GH + h : GH + h + 1, :])).astype(BF)
                key_grad, value_grad = state[h]
                out.append(
                    (
                        key_grad + dot_nn(slopes, queries),
                        value_grad + dot_nn(expo.astype(BF), backs),
                    )
                )
            return tuple(out)

        zero = jnp.zeros((WAYS, HD), F32)
        begin = tuple((zero, zero) for _ in range(GH))
        state = lax.fori_loop(lax.div(at_places[0], CHUNK // BLK), SEQ // CHUNK, chunk, begin)
        for h in range(GH):
            store_group(grad, own, head_columns(h), state[h][0].astype(BF))
            store_group(grad, own, head_columns(h, 1), state[h][1].astype(BF))
        return carry

    lax.fori_loop(0, 8 // GB, group, 0)


def call(kernel, operands, outs, scratch, cost, tabled=True):
    specs = [pl.BlockSpec(memory_space=VMEM)] * (len(operands) - int(tabled))
    if tabled:
        specs = [pl.BlockSpec(memory_space=SMEM)] + specs
    return pl.pallas_call(
        kernel,
        in_specs=specs,
        out_specs=[pl.BlockSpec(memory_space=VMEM)] * len(outs),
        out_shape=[jax.ShapeDtypeStruct(shape, kind) for shape, kind in outs],
        scratch_shapes=scratch,
        compiler_params=pltpu.CompilerParams(vmem_limit_bytes=40 * 2**20),
        cost_estimate=pl.CostEstimate(flops=cost, bytes_accessed=8 * 2**20, transcendentals=0),
    )(*operands)


HEAD_SCRATCH = VMEM((GH, SEQ, HD), BF)


def attend(tab, q, kv_own, kv_other):
    return call(
        forward_kernel,
        (tab, q, kv_own, kv_other),
        [((QROWS, GD), BF), ((QROWS, GD), F32), ((QROWS, 128), F32)],
        [HEAD_SCRATCH, VMEM((GH, SEQ, 128), BF)],
        10**8,
    )


def pack(back, exact, stats):
    return call(
        pack_kernel,
        (back, exact, stats),
        [((QROWS, 256), BF), ((QROWS, 128), F32)],
        [],
        10**7,
        tabled=False,
    )


def query_grads(tab, q, back, stats, kv_own, kv_other):
    return call(
        query_kernel,
        (tab, q, back, stats, kv_own, kv_other),
        [((QROWS, GD), BF)],
        [HEAD_SCRATCH, HEAD_SCRATCH],
        10**8,
    )[0]


def key_grads(tab, kv, q_all, x_all):
    pick = np.zeros((8, 128), np.float32)
    for j in range(2 * GH):
        for t in range(3):
            pick[j, GD - 128 + 3 * j + t] = 1.0
    return call(
        key_kernel,
        (tab, kv, q_all.reshape(SEQ, GD), x_all.reshape(SEQ, 256), jnp.asarray(pick, BF)),
        [((QROWS, 2 * GD), BF)],
        [HEAD_SCRATCH, HEAD_SCRATCH, VMEM((SEQ, 128), BF), VMEM((SEQ // CHUNK, 8, CHUNK), F32)],
        10**8,
    )[0]


def rest_kernel(att, two, down, branch, up, active, spread_t, fill_t, grad):
    def across(table, value):
        return dot_nt(table, value).astype(BF)

    two_t, down_t = across(spread_t[...], two[...]), across(spread_t[...], down[...])
    att_t = across(spread_t[...], att[...])
    last = active[:, D:]
    tops = ((two_t, up[:, :D]), (two_t, up[:, D:]), (down_t, active[:, :D]))
    for j, (left, right) in enumerate(tops):
        left = jnp.concatenate([left, across(fill_t[j], down[...])], axis=1)
        right = jnp.concatenate([right, last], axis=0)
        grad[:, j * D : (j + 1) * D] = dot_nn(left, right).astype(BF)
    grad[:, 3 * D :] = dot_nn(att_t, branch[...]).astype(BF)


def rest_grads(*rows):
    fills = np.stack([filling(j).T for j in range(3)])
    return call(
        rest_kernel,
        (*rows, jnp.asarray(widening().T, BF), jnp.asarray(fills, BF)),
        [((8 * 128, 7 * (D // 2)), BF)],
        [],
        10**8,
        tabled=False,
    )[0]


def place_table(pair_of_device):
    z, core = lax.axis_index("z"), lax.axis_index("c")
    pairs = pair_of_device.reshape(NX, NZ, NC).transpose(1, 2, 0)
    order = jnp.stack([z, (z + 3) % 4, (z + 1) % 4, (z + 2) % 4])
    plain = jnp.stack([pairs, NBLK - 1 - pairs], axis=-1).reshape(NBLK)
    pairs = jnp.take(pairs, order, axis=0)
    pairs = jnp.stack([jnp.take(pairs, core, axis=1), jnp.take(pairs, 1 - core, axis=1)])
    blocks = jnp.stack([pairs, NBLK - 1 - pairs], axis=-1).reshape(NBLK)
    own = blocks[: 2 * NX]
    rank = jnp.sum(own[:, None] > own[None, :], axis=1)
    hit = rank[None, :] == jnp.arange(2 * NX)[:, None]
    index = jnp.sum(jnp.where(hit, jnp.arange(2 * NX)[None, :], 0), axis=1)
    place = jnp.sum(jnp.where(hit, own[None, :], 0), axis=1)
    return jnp.concatenate([blocks, index, place, plain]).astype(jnp.int32)


def local(
    tokens,
    cotangent,
    pair_of_device,
    qkv_weight,
    out_weight,
    fc1_weight,
    fc2_weight,
    vectors,
    qkv_moment,
    qkv_second,
    out_moment,
    out_second,
    fc1_moment,
    fc1_second,
    fc2_moment,
    fc2_second,
    vector_moment,
    vector_second,
):
    xi, core = lax.axis_index("x"), lax.axis_index("c")
    everyone = ("x", "z", "c", "y")
    vector = vectors[0]
    tab = place_table(pair_of_device)
    widen = jnp.asarray(widening(), BF)

    mix = qkv_weight[0].astype(BF).reshape(6, 3, NX, GD).transpose(2, 0, 1, 3).reshape(NX, 1, 6, 3 * GD)
    mix = jnp.broadcast_to(mix, (NX, NY, 6, 3 * GD)).reshape(NX * NY, 6, 3 * GD)
    mix = lax.all_to_all(mix, ("x", "y"), 0, 0, tiled=True)
    mix = copy_gather(mix.reshape(NX * NY * 6, 3 * GD), ("z", "c"))
    mix = mix.reshape(NZ, NC, NX, NY, 6, 3 * GD).transpose(2, 0, 1, 3, 4, 5)
    tokens4 = ordered(ring_gather(tokens[0], "x"), "x")

    rest = jnp.concatenate([p[0].astype(BF) for p in (out_weight, fc1_weight, fc2_weight)], axis=1)
    rest = jnp.pad(rest, ((0, 2), (0, 0)))[None]
    rest, mix, tokens4 = lax.optimization_barrier((rest, mix, tokens4))
    rest_all = lax.all_gather(rest, everyone, axis=0, tiled=True).reshape(8 * 128, D + 2 * FF)

    w_mix = mix.reshape(D, 3 * GD)

    hidden4 = tokens4.astype(F32)
    normed4 = layer_norm(hidden4, vector[0], vector[1]).astype(BF)
    projected = jnp.dot(normed4, w_mix, preferred_element_type=F32)
    group_bias = lax.dynamic_slice_in_dim(vector[2:4], xi * GD, GD, 1)
    q4 = (projected[:, :GD] + group_bias[0]).astype(BF)
    k4 = projected[:, GD : 2 * GD].astype(BF)
    v4 = (projected[:, 2 * GD :] + group_bias[1]).astype(BF)
    kv4 = jnp.concatenate([k4, v4], axis=1)
    kv_own, kv_other = gather_zc(kv4)
    q_in, _ = lax.optimization_barrier((q4, kv_other))
    q_all = copy_gather(q_in, ("z", "c"))
    att4, exact4, stats4 = attend(tab, q4, kv_own, kv_other)
    att4, q_all = lax.optimization_barrier((att4, q_all))

    attended = lax.all_to_all(att4.reshape(NX, ROWS, GD), "x", 0, 0, tiled=True)
    attended = attended.transpose(1, 0, 2).reshape(ROWS, D)

    w_out, w_up, w_down = rest_all[:, :D], rest_all[:, D : D + FF], rest_all[:, D + FF :]

    def wide(value):
        return jnp.dot(value, widen, preferred_element_type=F32).astype(BF)

    def narrow(value):
        return lax.dot_general(
            value, widen.astype(F32), (((1,), (1,)), ((), ())), precision=lax.Precision.HIGHEST
        )

    hidden = tokens[0].astype(F32)
    middle = hidden + jnp.dot(wide(attended), w_out, preferred_element_type=F32) + vector[4]
    normed_two = layer_norm(middle, vector[5], vector[6]).astype(BF)
    down_low = cotangent[0]
    back_active = jnp.dot(wide(down_low), w_down, preferred_element_type=F32)
    pre_active = jnp.dot(wide(normed_two), w_up, preferred_element_type=F32) + vector[8:12].reshape(FF)
    active_wide, gelu_back = jax.vjp(jax.nn.gelu, pre_active)
    active = active_wide.astype(BF)
    up_low = gelu_back(back_active)[0].astype(BF)
    back_two = narrow(dot_nt(up_low, w_up))

    gradient = cotangent[0].astype(F32)
    _, norm_back = jax.vjp(layer_norm, middle, vector[5], vector[6])
    back_middle, gain_two, shift_two = norm_back(back_two)
    gradient = gradient + back_middle
    branch_low = gradient.astype(BF)
    back_attended = dot_nt(branch_low, w_out).astype(BF)
    back_attended = dot_nt(back_attended, widen).astype(BF)
    back4 = lax.all_to_all(
        back_attended.reshape(ROWS, NX, GD).transpose(1, 0, 2), "x", 0, 0, tiled=True
    ).reshape(QROWS, GD)
    packed, stats_all = pack(back4, exact4, stats4)
    x_all = copy_gather(packed, ("z", "c"))

    late, _ = lax.optimization_barrier(
        ((attended, normed_two, down_low, branch_low, up_low, active), packed)
    )

    def outer(left, right):
        return jnp.einsum("rc,re->ce", left, right, preferred_element_type=F32).astype(BF)

    def half_of(value, which):
        size = value.shape[1] // 2
        return lax.dynamic_slice_in_dim(value, which * size, size, 1)

    mine = list(late[:3]) + [half_of(v, core) for v in late[3:]]
    theirs = list(late[:3]) + [half_of(v, 1 - core) for v in late[3:]]
    got = lax.ppermute(jnp.concatenate(theirs, axis=1), "c", SWAP)
    at, both = 0, []
    for value in mine:
        both.append(jnp.concatenate([value, got[:, at : at + value.shape[1]]], axis=0))
        at = at + value.shape[1]
    rest_grad = rest_grads(*both).reshape(128, 8, 7 * (D // 2))

    down_out = narrow(dot_nt(active, w_down))
    block_out = middle + down_out + vector[7]

    back_in, rest_grad = lax.optimization_barrier((back4, rest_grad))
    rest_grad = lax.all_to_all(rest_grad, everyone, 0, 0, tiled=True)
    wide4, back_in = lax.optimization_barrier((wide(normed4), back_in))
    back_q4 = query_grads(tab, q4, back_in, stats_all, kv_own, kv_other)
    back_q4, x_all = lax.optimization_barrier((back_q4, x_all))
    back_kv4 = key_grads(tab, kv4, q_all, x_all)
    back_kv4, rest_grad = lax.optimization_barrier((back_kv4, rest_grad))
    mixed4 = jnp.concatenate([back_q4, back_kv4], axis=1)

    mix_grad = outer(wide4, mixed4).reshape(128, 8, 3 * GD)
    mix_grad, mixed4 = lax.optimization_barrier((mix_grad, mixed4))
    mix_grad = lax.all_to_all(mix_grad, everyone, 0, 0, tiled=True)
    back_normed4 = dot_nt(mixed4, w_mix)
    _, shift_back = jax.vjp(
        lambda gain, shift: layer_norm(hidden4, gain, shift), vector[0], vector[1]
    )
    gain_one, shift_one = shift_back(back_normed4)
    pieces = lax.all_to_all(
        back_normed4.astype(BF).reshape(NX, ROWS, D), "x", 0, 0, tiled=True
    )

    def column_sum(value):
        return jnp.sum(value.astype(F32), axis=0)

    def at_group(value):
        return lax.dynamic_update_slice_in_dim(jnp.zeros((D,), F32), value, xi * GD, 0)

    vector_grad = jnp.concatenate(
        [
            jnp.stack(
                [
                    gain_one,
                    shift_one,
                    at_group(column_sum(back_q4)),
                    at_group(column_sum(back_kv4[:, GD:])),
                    column_sum(branch_low),
                    gain_two,
                    shift_two,
                    column_sum(down_low),
                ]
            ),
            column_sum(up_low).reshape(4, D),
        ]
    )
    vector_near = copy_gather(vector_grad, ("c", "y"))
    mix_grad, pieces, vector_near = lax.optimization_barrier((mix_grad, pieces, vector_near))
    vector_total = jnp.sum(
        copy_gather(jnp.sum(vector_near, axis=0), ("x", "z")), axis=0
    )[None]

    back_normed = jnp.sum(pieces.astype(F32), axis=0)
    _, first_back = jax.vjp(lambda h: layer_norm(h, vector[0], vector[1]), hidden)
    input_grad = gradient + first_back(back_normed)[0]

    mix_grad = jnp.sum(mix_grad.reshape(NX, 32, 8, 3 * GD)[:, :, :6].astype(F32), axis=1)
    mix_grad = (
        mix_grad.reshape(NX, 6, 3, GD).transpose(1, 2, 0, 3).reshape(1, 6, 3 * D)
    )
    half = FF // 2
    wide_sum = jnp.sum(
        rest_grad.reshape(NX * NZ, NC, NY, 8, rest_grad.shape[2]).astype(F32), axis=(0, 2)
    )
    top, fill = wide_sum[:, :6], wide_sum[:, 6:, : 3 * D].reshape(NC, 6, D)

    def joined(*parts):
        return jnp.concatenate([part[j] for j in range(NC) for part in parts], axis=1)[None]

    out_grad = joined(top[:, :, 3 * D :])
    fc1_grad = joined(top[:, :, : 2 * D])
    fc2_grad = joined(top[:, :, 2 * D : 3 * D], fill)

    qkv_new = adamw(qkv_weight, qkv_moment, qkv_second, mix_grad, RATE_MATRIX, DECAY_MATRIX)
    out_new = adamw(
        out_weight, out_moment, out_second, out_grad, RATE_MATRIX, DECAY_MATRIX
    )
    fc1_new = adamw(
        fc1_weight, fc1_moment, fc1_second, fc1_grad, RATE_MATRIX, DECAY_MATRIX
    )
    fc2_new = adamw(
        fc2_weight, fc2_moment, fc2_second, fc2_grad, RATE_MATRIX, DECAY_MATRIX
    )
    vec_new = adamw(vectors, vector_moment, vector_second, vector_total, RATE_VECTOR, 0.0)
    return (
        block_out[None],
        input_grad[None],
        *qkv_new,
        *out_new,
        *fc1_new,
        *fc2_new,
        *vec_new,
    )


def solution(mesh):
    grid = Mesh(mesh.devices.reshape(NX, NZ, NC, NY), ("x", "z", "c", "y"))
    rows = P("y", ("x", "z", "c"), None)
    weight = P(None, ("x", "z", "c", "y"), None)
    in_specs = (rows, rows, P()) + (weight,) * 4 + (P(),) + (weight,) * 8 + (P(), P())
    out_specs = (rows, rows) + (weight,) * 12 + (P(), P(), P())
    return jax.shard_map(local, mesh=grid, in_specs=in_specs, out_specs=out_specs, check_vma=False)
```

```python
import jax
import jax.numpy as jnp
import numpy as np
from jax import lax
from jax.experimental import pallas as pl
from jax.experimental.pallas import tpu as pltpu
from jax.sharding import Mesh
from jax.sharding import PartitionSpec as P

D = 768
HEADS = 12
HD = 64
FF = 3072
LAYERS = 1
STEP = 5

EPS_NORM = 1e-05
NEGATIVE = -1e30
BETA_ONE = 0.9
BETA_TWO = 0.999
RATE_MATRIX = 0.1
RATE_VECTOR = 0.5
DECAY_MATRIX = 0.1
EPS_ADAM = 1e-08

NX = 4
NZ = 4
NC = 2
NY = 4
GH = HEADS // NX
GD = GH * HD
ROWS = 128
BLK = 64
QROWS = NX * ROWS
SEQ = 4096
NBLK = SEQ // BLK
CHUNK = 1024
GB = 4
WAYS = BLK * GB
BF = jnp.bfloat16
F32 = jnp.float32
VMEM = pltpu.VMEM
SMEM = pltpu.SMEM


def layer_norm(hidden, norm_gain, norm_shift):
    center = hidden - jnp.mean(hidden, axis=-1, keepdims=True)
    spread = jnp.mean(center * center, axis=-1, keepdims=True)
    return center * lax.rsqrt(spread + EPS_NORM) * norm_gain + norm_shift


def adamw(weight, moment, second, gradient, step_rate, decay_rate):
    moment_new = BETA_ONE * moment + (1.0 - BETA_ONE) * gradient
    second_new = BETA_TWO * second + (1.0 - BETA_TWO) * gradient * gradient
    moment_hat = moment_new / (1.0 - BETA_ONE**STEP)
    second_hat = second_new / (1.0 - BETA_TWO**STEP)
    weight_new = weight - step_rate * (
        moment_hat / (jnp.sqrt(second_hat) + EPS_ADAM) + decay_rate * weight
    )
    return (moment_new, second_new, weight_new)


RIGHT = [(i, (i + 1) % 4) for i in range(4)]
LEFT = [(i, (i + 3) % 4) for i in range(4)]
SWAP = [(0, 1), (1, 0)]
EVEN = [(0, 1), (1, 0), (2, 3), (3, 2)]
ODD = [(1, 2), (2, 1), (3, 0), (0, 3)]


def ring_gather(part, axis):
    half = part.shape[0] // 2
    before = lax.ppermute(part, axis, RIGHT)
    after = lax.ppermute(part, axis, LEFT)
    far_low = lax.ppermute(before[:half], axis, RIGHT)
    far_high = lax.ppermute(after[half:], axis, LEFT)
    return jnp.concatenate([part, before, after, far_low, far_high], axis=0)


def ordered(gathered, axis):
    rows = gathered.shape[0] // 4
    me = lax.axis_index(axis)
    relative = lax.rem(4 + jnp.arange(4) - me, 4)
    slot = jnp.where(relative == 1, 2, jnp.where(relative == 2, 3, jnp.where(relative == 3, 1, 0)))
    return jnp.take(gathered.reshape(4, rows, -1), slot, axis=0).reshape(gathered.shape)


def gather_zc(part):
    own = ring_gather(part, "z")
    return own, lax.ppermute(own, "c", SWAP)


def copy_gather(part, axes):
    count = lax.axis_size(axes)
    return lax.all_to_all(jnp.broadcast_to(part[None], (count,) + part.shape), axes, 0, 0, tiled=True)


def sum_ring(value, axis):
    value = value + lax.ppermute(value, axis, EVEN)
    return value + lax.ppermute(value, axis, ODD)


def widening():
    pick = np.zeros((D, 8 * 128), np.float32)
    feature = np.arange(D)
    pick[feature, feature // 6 * 8 + feature % 6] = 1.0
    return pick


def filling(part):
    pick = np.zeros((D, 8 * 128), np.float32)
    device = np.arange(128)
    pick[6 * device + part, 8 * device + 6] = 1.0
    pick[6 * device + 3 + part, 8 * device + 7] = 1.0
    return pick


def dot_nt(left, right):
    return lax.dot_general(left, right, (((1,), (1,)), ((), ())), preferred_element_type=F32)


def dot_nn(left, right):
    return lax.dot_general(left, right, (((1,), (0,)), ((), ())), preferred_element_type=F32)


def group_rows(ref, blocks, columns):
    return jnp.concatenate(
        [ref[pl.ds(pl.multiple_of(block * BLK, BLK), BLK), columns] for block in blocks], axis=0
    )


def store_group(ref, blocks, columns, value):
    for at, block in enumerate(blocks):
        rows = slice(at * BLK, (at + 1) * BLK)
        ref[pl.ds(pl.multiple_of(block * BLK, BLK), BLK), columns] = value[rows]


def group_places(blocks, shape, axis):
    index = lax.broadcasted_iota(jnp.int32, shape, axis)
    places = blocks[0] * BLK + index
    for at in range(1, len(blocks)):
        places = jnp.where(index < at * BLK, places, (blocks[at] - at) * BLK + index)
    return places


def group_of(tab, g):
    own = [tab[NBLK + GB * g + j] for j in range(GB)]
    return own, [tab[NBLK + 8 + GB * g + j] for j in range(GB)]


def sort_blocks(tab, sources, store):
    at = 0
    for source in sources:
        count = source.shape[0] // BLK

        def move(block, carry, source=source, at=at):
            place = tab[at + block]
            rows = source[pl.ds(pl.multiple_of(block * BLK, BLK), BLK), :]
            store(pl.multiple_of(place * BLK, BLK), rows)
            return carry

        lax.fori_loop(0, count, move, 0)
        at = at + count


def head_columns(head, part=0):
    return slice(part * GD + head * HD, part * GD + (head + 1) * HD)


def forward_kernel(tab, q, kv_own, kv_other, att, exact, stats, k_s, v_s):
    def store(at, rows):
        ones = jnp.ones((BLK, HD), BF)
        for head in range(GH):
            k_s[head, pl.ds(at, BLK), :] = rows[:, head_columns(head)]
            v_s[head, pl.ds(at, BLK), :] = jnp.concatenate(
                [rows[:, head_columns(head, 1)], ones], axis=1
            )

    sort_blocks(tab, (kv_own, kv_other), store)
    lane = lax.broadcasted_iota(jnp.int32, (WAYS, 128), 1)

    def group(g, carry):
        own, at_places = group_of(tab, g)
        places = group_places(at_places, (WAYS, 1), 0)
        queries = [
            group_rows(q, own, head_columns(h)) * jnp.asarray(0.125, BF)
            for h in range(GH)
        ]

        def chunk(at, state):
            start = pl.multiple_of(at * CHUNK, CHUNK)
            keys_at = start + lax.broadcasted_iota(jnp.int32, (WAYS, CHUNK), 1)
            allowed = keys_at <= places
            out = []
            for h in range(GH):
                peak, plain, extra = state[h]
                scores = dot_nt(queries[h], k_s[h, pl.ds(start, CHUNK), :])
                scores = jnp.where(allowed, scores, NEGATIVE)
                peak_new = jnp.maximum(peak, jnp.max(scores, axis=1, keepdims=True))
                shrink = jnp.exp(peak - peak_new)
                expo = jnp.exp(scores - peak_new)
                probs = expo.astype(BF)
                residue = (expo - probs.astype(F32)).astype(BF)
                values = v_s[h, pl.ds(start, CHUNK), :]
                plain = plain * shrink + dot_nn(probs, values)
                extra = extra * shrink + dot_nn(residue, values)
                out.append((peak_new, plain, extra))
            return tuple(out)

        zero = jnp.zeros((WAYS, 128), F32)
        begin = tuple((jnp.full((WAYS, 1), NEGATIVE, F32), zero, zero) for _ in range(GH))
        state = lax.fori_loop(0, lax.div(at_places[-1], CHUNK // BLK) + 1, chunk, begin)
        table = jnp.zeros((WAYS, 128), F32)
        for h in range(GH):
            peak, plain, extra = state[h]
            both = plain + extra
            mass = both[:, HD : HD + 1]
            store_group(att, own, head_columns(h), (plain[:, :HD] / mass).astype(BF))
            store_group(exact, own, head_columns(h), both[:, :HD] / mass)
            table = jnp.where(lane == h, peak + jnp.log(mass), table)
        store_group(stats, own, slice(0, 128), table)
        return carry

    lax.fori_loop(0, 8 // GB, group, 0)


def pack_kernel(back, exact, stats_in, q, packed, stats):
    lane = lax.broadcasted_iota(jnp.int32, (QROWS, 128), 1)
    table = stats_in[...]
    extra = jnp.zeros((QROWS, 128), F32)
    for h in range(GH):
        columns = head_columns(h)
        dot = jnp.sum(back[:, columns].astype(F32) * exact[:, columns], axis=1, keepdims=True)
        table = jnp.where(lane == GH + h, dot, table)
    stats[...] = table
    for j in range(2 * GH):
        value = table[:, j : j + 1]
        for t in range(3):
            piece = value.astype(BF).astype(F32)
            value = value - piece
            extra = jnp.where(lane == 3 * j + t, piece, extra)
    packed[:, :GD] = back[...]
    packed[:, GD:256] = extra[:, : 256 - GD].astype(BF)
    packed[:, 256:] = jnp.concatenate([q[...], jnp.zeros((QROWS, 256 - GD), BF)], axis=1)


def query_kernel(tab, q, back, stats, kv_own, kv_other, grad, k_s, v_s):
    def store(at, rows):
        for head in range(GH):
            k_s[head, pl.ds(at, BLK), :] = rows[:, head_columns(head)]
            v_s[head, pl.ds(at, BLK), :] = rows[:, head_columns(head, 1)]

    sort_blocks(tab, (kv_own, kv_other), store)

    def group(g, carry):
        own, at_places = group_of(tab, g)
        places = group_places(at_places, (WAYS, 1), 0)
        table = group_rows(stats, own, slice(0, 128))
        queries = [
            group_rows(q, own, head_columns(h)) * jnp.asarray(0.125, BF)
            for h in range(GH)
        ]
        backs = [group_rows(back, own, head_columns(h)) for h in range(GH)]

        def chunk(at, state):
            start = pl.multiple_of(at * CHUNK, CHUNK)
            keys_at = start + lax.broadcasted_iota(jnp.int32, (WAYS, CHUNK), 1)
            allowed = keys_at <= places
            out = []
            for h in range(GH):
                keys = k_s[h, pl.ds(start, CHUNK), :]
                scores = dot_nt(queries[h], keys) - table[:, h : h + 1]
                expo = jnp.exp(jnp.where(allowed, scores, NEGATIVE))
                dots = dot_nt(backs[h], v_s[h, pl.ds(start, CHUNK), :])
                slopes = (expo * (dots - table[:, GH + h : GH + h + 1])).astype(BF)
                out.append(state[h] + dot_nn(slopes, keys))
            return tuple(out)

        begin = tuple(jnp.zeros((WAYS, HD), F32) for _ in range(GH))
        state = lax.fori_loop(0, lax.div(at_places[-1], CHUNK // BLK) + 1, chunk, begin)
        for h in range(GH):
            store_group(grad, own, head_columns(h), (state[h] * 0.125).astype(BF))
        return carry

    lax.fori_loop(0, 8 // GB, group, 0)


def key_kernel(tab, kv, x_own, x_other, pick, grad, q_s, d_s, r_s, row_s):
    def store(at, rows):
        for head in range(GH):
            d_s[head, pl.ds(at, BLK), :] = rows[:, head_columns(head)]
            q_s[head, pl.ds(at, BLK), :] = rows[
                :, 256 + head * HD : 256 + (head + 1) * HD
            ] * jnp.asarray(0.125, BF)
        r_s[pl.ds(at, BLK), :] = rows[:, 128:256]

    sort_blocks(tab, (x_own, x_other), store)

    def rows_of(at, carry):
        start = pl.multiple_of(at * CHUNK, CHUNK)
        row_s[at] = dot_nt(pick[...], r_s[pl.ds(start, CHUNK), :])
        return carry

    lax.fori_loop(0, SEQ // CHUNK, rows_of, 0)

    def group(g, carry):
        own, at_places = group_of(tab, g)
        places = group_places(at_places, (WAYS, 1), 0)
        keys = [group_rows(kv, own, head_columns(h)) for h in range(GH)]
        values = [group_rows(kv, own, head_columns(h, 1)) for h in range(GH)]

        def chunk(at, state):
            start = pl.multiple_of(at * CHUNK, CHUNK)
            queries_at = start + lax.broadcasted_iota(jnp.int32, (WAYS, CHUNK), 1)
            allowed = places <= queries_at
            rows = row_s[at]
            out = []
            for h in range(GH):
                queries = q_s[h, pl.ds(start, CHUNK), :]
                backs = d_s[h, pl.ds(start, CHUNK), :]
                scores = dot_nt(keys[h], queries) - rows[h : h + 1, :]
                expo = jnp.exp(jnp.where(allowed, scores, NEGATIVE))
                dots = dot_nt(values[h], backs)
                slopes = (expo * (dots - rows[GH + h : GH + h + 1, :])).astype(BF)
                key_grad, value_grad = state[h]
                out.append(
                    (
                        key_grad + dot_nn(slopes, queries),
                        value_grad + dot_nn(expo.astype(BF), backs),
                    )
                )
            return tuple(out)

        zero = jnp.zeros((WAYS, HD), F32)
        begin = tuple((zero, zero) for _ in range(GH))
        state = lax.fori_loop(lax.div(at_places[0], CHUNK // BLK), SEQ // CHUNK, chunk, begin)
        for h in range(GH):
            store_group(grad, own, head_columns(h), state[h][0].astype(BF))
            store_group(grad, own, head_columns(h, 1), state[h][1].astype(BF))
        return carry

    lax.fori_loop(0, 8 // GB, group, 0)


def call(kernel, operands, outs, scratch, cost, tabled=True):
    specs = [pl.BlockSpec(memory_space=VMEM)] * (len(operands) - int(tabled))
    if tabled:
        specs = [pl.BlockSpec(memory_space=SMEM)] + specs
    return pl.pallas_call(
        kernel,
        in_specs=specs,
        out_specs=[pl.BlockSpec(memory_space=VMEM)] * len(outs),
        out_shape=[jax.ShapeDtypeStruct(shape, kind) for shape, kind in outs],
        scratch_shapes=scratch,
        compiler_params=pltpu.CompilerParams(vmem_limit_bytes=40 * 2**20),
        cost_estimate=pl.CostEstimate(flops=cost, bytes_accessed=8 * 2**20, transcendentals=0),
    )(*operands)


HEAD_SCRATCH = VMEM((GH, SEQ, HD), BF)


def attend(tab, q, kv_own, kv_other):
    return call(
        forward_kernel,
        (tab, q, kv_own, kv_other),
        [((QROWS, GD), BF), ((QROWS, GD), F32), ((QROWS, 128), F32)],
        [HEAD_SCRATCH, VMEM((GH, SEQ, 128), BF)],
        23 * 10**9,
    )


def pack(back, exact, stats, q):
    return call(
        pack_kernel,
        (back, exact, stats, q),
        [((QROWS, 512), BF), ((QROWS, 128), F32)],
        [],
        10**7,
        tabled=False,
    )


def query_grads(tab, q, back, stats, kv_own, kv_other):
    return call(
        query_kernel,
        (tab, q, back, stats, kv_own, kv_other),
        [((QROWS, GD), BF)],
        [HEAD_SCRATCH, HEAD_SCRATCH],
        18 * 10**9,
    )[0]


def key_grads(tab, kv, x_own, x_other):
    pick = np.zeros((8, 128), np.float32)
    for j in range(2 * GH):
        for t in range(3):
            pick[j, GD - 128 + 3 * j + t] = 1.0
    return call(
        key_kernel,
        (tab, kv, x_own, x_other, jnp.asarray(pick, BF)),
        [((QROWS, 2 * GD), BF)],
        [HEAD_SCRATCH, HEAD_SCRATCH, VMEM((SEQ, 128), BF), VMEM((SEQ // CHUNK, 8, CHUNK), F32)],
        24 * 10**9,
    )[0]


def block_kernel(
    att, tok, cot, vec, w, widen, block_out, grad, two, low, up, active, back_att, sums
):
    def wide(value):
        return dot_nn(value, widen[...]).astype(BF)

    def narrow(value):
        total = None
        for _ in range(3):
            piece = value.astype(BF)
            value = value - piece.astype(F32)
            part = dot_nt(piece, widen[...])
            total = part if total is None else total + part
        return total

    def row(j):
        return vec[j : j + 1, :]

    attended = jnp.concatenate([att[g] for g in range(NX)], axis=1)
    middle = tok[...].astype(F32) + dot_nn(wide(attended), w[:, :D]) + row(4)
    center = middle - jnp.mean(middle, axis=1, keepdims=True)
    inverse = lax.rsqrt(jnp.mean(center * center, axis=1, keepdims=True) + EPS_NORM)
    unit = center * inverse
    normed_two = (unit * row(5) + row(6)).astype(BF)
    two[...] = normed_two
    wide_two, wide_down = wide(normed_two), wide(cot[...])
    back_two = jnp.zeros((ROWS, 8 * 128), F32)
    down = jnp.zeros((ROWS, 8 * 128), F32)
    slope = (2.0 / np.pi) ** 0.5
    for j in range(FF // D):
        w_up = w[:, D * (1 + j) : D * (2 + j)]
        w_down = w[:, D + FF + D * j : D + FF + D * (j + 1)]
        pre = dot_nn(wide_two, w_up) + row(8 + j)
        back_active = dot_nn(wide_down, w_down)
        square = pre * pre
        bend = jnp.tanh(slope * (pre + 0.044715 * (square * pre)))
        half = 0.5 * (1.0 + bend)
        rate = half + 0.5 * pre * (1.0 - bend * bend) * (slope * (1.0 + 3 * 0.044715 * square))
        act_low = (pre * half).astype(BF)
        up_low = (back_active * rate).astype(BF)
        active[:, j * D : (j + 1) * D] = act_low
        up[:, j * D : (j + 1) * D] = up_low
        sums[4 + j : 5 + j, :] = jnp.sum(up_low.astype(F32), axis=0, keepdims=True)
        back_two = back_two + dot_nt(up_low, w_up)
        down = down + dot_nt(act_low, w_down)
    back_two = narrow(back_two)
    back_unit = back_two * row(5)
    back_middle = inverse * (
        back_unit
        - jnp.mean(back_unit, axis=1, keepdims=True)
        - unit * jnp.mean(back_unit * unit, axis=1, keepdims=True)
    )
    gradient = cot[...].astype(F32) + back_middle
    grad[...] = gradient
    branch_low = gradient.astype(BF)
    low[...] = branch_low
    back = dot_nt(dot_nt(branch_low, w[:, :D]).astype(BF), widen[...]).astype(BF)
    for g in range(NX):
        back_att[g] = back[:, g * GD : (g + 1) * GD]
    block_out[...] = middle + narrow(down) + row(7)
    sums[0:1, :] = jnp.sum(branch_low.astype(F32), axis=0, keepdims=True)
    sums[1:2, :] = jnp.sum(back_two * unit, axis=0, keepdims=True)
    sums[2:3, :] = jnp.sum(back_two, axis=0, keepdims=True)
    sums[3:4, :] = jnp.sum(cot[...].astype(F32), axis=0, keepdims=True)


def feed_forward(*operands):
    return call(
        block_kernel,
        operands,
        [
            ((ROWS, D), F32),
            ((ROWS, D), F32),
            ((ROWS, D), BF),
            ((ROWS, D), BF),
            ((ROWS, FF), BF),
            ((ROWS, FF), BF),
            ((NX, ROWS, GD), BF),
            ((8, D), F32),
        ],
        [],
        20 * 10**9,
        tabled=False,
    )


def rest_kernel(att, two, down, branch, up, active, spread_t, fill_t, grad):
    def across(table, value):
        return dot_nt(table, value).astype(BF)

    two_t, down_t = across(spread_t[...], two[...]), across(spread_t[...], down[...])
    att_t = across(spread_t[...], att[...])
    last = active[:, D:]
    tops = ((two_t, up[:, :D]), (two_t, up[:, D:]), (down_t, active[:, :D]))
    for j, (left, right) in enumerate(tops):
        left = jnp.concatenate([left, across(fill_t[j], down[...])], axis=1)
        right = jnp.concatenate([right, last], axis=0)
        grad[:, j * D : (j + 1) * D] = dot_nn(left, right).astype(BF)
    grad[:, 3 * D :] = dot_nn(att_t, branch[...]).astype(BF)


def rest_grads(*rows):
    fills = np.stack([filling(j).T for j in range(3)])
    return call(
        rest_kernel,
        (*rows, jnp.asarray(widening().T, BF), jnp.asarray(fills, BF)),
        [((8 * 128, 7 * (D // 2)), BF)],
        [],
        9 * 10**9,
        tabled=False,
    )[0]


def place_table(pair_of_device):
    z, core = lax.axis_index("z"), lax.axis_index("c")
    pairs = pair_of_device.reshape(NX, NZ, NC).transpose(1, 2, 0)
    order = jnp.stack([z, (z + 3) % 4, (z + 1) % 4, (z + 2) % 4])
    pairs = jnp.take(pairs, order, axis=0)
    pairs = jnp.stack([jnp.take(pairs, core, axis=1), jnp.take(pairs, 1 - core, axis=1)])
    blocks = jnp.stack([pairs, NBLK - 1 - pairs], axis=-1).reshape(NBLK)
    own = blocks[: 2 * NX]
    rank = jnp.sum(own[:, None] > own[None, :], axis=1)
    hit = rank[None, :] == jnp.arange(2 * NX)[:, None]
    index = jnp.sum(jnp.where(hit, jnp.arange(2 * NX)[None, :], 0), axis=1)
    place = jnp.sum(jnp.where(hit, own[None, :], 0), axis=1)
    return jnp.concatenate([blocks, index, place]).astype(jnp.int32)


def local(
    tokens,
    cotangent,
    pair_of_device,
    qkv_weight,
    out_weight,
    fc1_weight,
    fc2_weight,
    vectors,
    qkv_moment,
    qkv_second,
    out_moment,
    out_second,
    fc1_moment,
    fc1_second,
    fc2_moment,
    fc2_second,
    vector_moment,
    vector_second,
):
    xi, core = lax.axis_index("x"), lax.axis_index("c")
    everyone = ("x", "z", "c", "y")
    vector = vectors[0]
    tab = place_table(pair_of_device)
    widen = jnp.asarray(widening(), BF)

    mix = qkv_weight[0].astype(BF).reshape(6, 3, NX, GD).transpose(2, 0, 1, 3).reshape(NX, 1, 6, 3 * GD)
    mix = jnp.broadcast_to(mix, (NX, NY, 6, 3 * GD)).reshape(NX * NY, 6, 3 * GD)
    mix = lax.all_to_all(mix, ("x", "y"), 0, 0, tiled=True)
    mix = copy_gather(mix.reshape(NX * NY * 6, 3 * GD), ("z", "c"))
    mix = mix.reshape(NZ, NC, NX, NY, 6, 3 * GD).transpose(2, 0, 1, 3, 4, 5)
    tokens4 = ordered(ring_gather(tokens[0], "x"), "x")

    rest = jnp.concatenate([p[0].astype(BF) for p in (out_weight, fc1_weight, fc2_weight)], axis=1)
    rest = jnp.pad(rest, ((0, 2), (0, 0)))[None]
    rest, mix, tokens4 = lax.optimization_barrier((rest, mix, tokens4))
    rest_all = lax.all_gather(rest, everyone, axis=0, tiled=True).reshape(8 * 128, D + 2 * FF)

    w_mix = mix.reshape(D, 3 * GD)

    hidden4 = tokens4.astype(F32)
    normed4 = layer_norm(hidden4, vector[0], vector[1]).astype(BF)
    projected = jnp.dot(normed4, w_mix, preferred_element_type=F32)
    group_bias = lax.dynamic_slice_in_dim(vector[2:4], xi * GD, GD, 1)
    q4 = (projected[:, :GD] + group_bias[0]).astype(BF)
    k4 = projected[:, GD : 2 * GD].astype(BF)
    v4 = (projected[:, 2 * GD :] + group_bias[1]).astype(BF)
    kv4 = jnp.concatenate([k4, v4], axis=1)
    wide4 = jnp.dot(normed4, widen, preferred_element_type=F32).astype(BF)
    kv_own, kv_other = gather_zc(kv4)
    q4, wide4 = lax.optimization_barrier((q4, wide4))
    att4, exact4, stats4 = attend(tab, q4, kv_own, kv_other)
    attended = lax.all_to_all(att4.reshape(NX, ROWS, GD), "x", 0, 0, tiled=True)
    block_out, gradient, normed_two, branch_low, up_low, active, back_attended, early_rows = (
        feed_forward(attended, tokens[0], cotangent[0], vector, rest_all, widen)
    )
    attended = attended.transpose(1, 0, 2).reshape(ROWS, D)
    down_low = cotangent[0]
    back4 = lax.all_to_all(back_attended, "x", 0, 0, tiled=True).reshape(QROWS, GD)
    packed, stats_all = pack(back4, exact4, stats4, q4)
    x_own = ring_gather(packed, "z")
    x_other = lax.ppermute(x_own, "c", SWAP)

    late, _ = lax.optimization_barrier(
        ((attended, normed_two, down_low, branch_low, up_low, active), packed)
    )

    def outer(left, right):
        return jnp.einsum("rc,re->ce", left, right, preferred_element_type=F32).astype(BF)

    def half_of(value, which):
        size = value.shape[1] // 2
        return lax.dynamic_slice_in_dim(value, which * size, size, 1)

    mine = list(late[:3]) + [half_of(v, core) for v in late[3:]]
    theirs = list(late[:3]) + [half_of(v, 1 - core) for v in late[3:]]
    got = lax.ppermute(jnp.concatenate(theirs, axis=1), "c", SWAP)
    at, both = 0, []
    for value in mine:
        both.append(jnp.concatenate([value, got[:, at : at + value.shape[1]]], axis=0))
        at = at + value.shape[1]
    rest_grad, back_in = lax.optimization_barrier((rest_grads(*both), back4))
    rest_grad = lax.psum_scatter(rest_grad, "x", scatter_dimension=0, tiled=True)

    back_q4 = query_grads(tab, q4, back_in, stats_all, kv_own, kv_other)
    back_kv4 = key_grads(tab, kv4, x_own, x_other)
    mixed4 = jnp.concatenate([back_q4, back_kv4], axis=1)

    mix_grad = outer(wide4, mixed4).reshape(NX, 32, 8, 3 * GD).transpose(1, 2, 0, 3)
    joint = jnp.concatenate(
        [mix_grad.reshape(32, 8, 3 * D), rest_grad.reshape(32, 8, rest_grad.shape[1])], axis=2
    )
    joint = lax.all_to_all(joint, ("z", "c", "y"), 0, 0, tiled=True)
    back_normed4 = dot_nt(mixed4, w_mix)
    _, shift_back = jax.vjp(
        lambda gain, shift: layer_norm(hidden4, gain, shift), vector[0], vector[1]
    )
    gain_one, shift_one = shift_back(back_normed4)
    pieces = back_normed4.astype(BF)

    def piece_of(device):
        return lax.dynamic_slice_in_dim(pieces, lax.rem(device, NX) * ROWS, ROWS, 0)

    back_normed = lax.dynamic_slice_in_dim(back_normed4, xi * ROWS, ROWS, 0)
    for step in (1, 2, 3):
        moved = lax.ppermute(piece_of(xi + step), "x", [(i, (i + step) % 4) for i in range(4)])
        back_normed = back_normed + moved.astype(F32)

    def column_sum(value):
        return jnp.sum(value.astype(F32), axis=0)

    def at_group(value):
        return lax.dynamic_update_slice_in_dim(jnp.zeros((D,), F32), value, xi * GD, 0)

    late_rows = jnp.stack(
        [
            gain_one,
            shift_one,
            at_group(column_sum(back_q4)),
            at_group(column_sum(back_kv4[:, GD:])),
        ]
    )
    vector_part = jnp.concatenate([late_rows, early_rows], axis=0)
    vector_part = vector_part + lax.ppermute(vector_part, "c", SWAP)
    vector_part = sum_ring(vector_part, "y")
    joint, vector_part = lax.optimization_barrier((joint, vector_part))
    vector_total = sum_ring(sum_ring(vector_part, "z"), "x")[None]

    hidden = tokens[0].astype(F32)
    _, first_back = jax.vjp(lambda h: layer_norm(h, vector[0], vector[1]), hidden)
    input_grad = gradient + first_back(back_normed)[0]

    mix_grad = jnp.sum(joint[:, :, : 3 * D].astype(F32), axis=0).astype(BF)
    mix_grad = lax.all_to_all(
        mix_grad.reshape(8, NX, 3 * GD).transpose(1, 0, 2), "x", 0, 0, tiled=True
    )[:, :6].astype(F32)
    mix_grad = (
        mix_grad.reshape(NX, 6, 3, GD).transpose(1, 2, 0, 3).reshape(1, 6, 3 * D)
    )
    wide_sum = jnp.sum(
        joint[:, :, 3 * D :].reshape(NZ, NC, NY, 8, 7 * (D // 2)).astype(F32), axis=(0, 2)
    )
    top, fill = wide_sum[:, :6], wide_sum[:, 6:, : 3 * D].reshape(NC, 6, D)

    def joined(*parts):
        return jnp.concatenate([part[j] for j in range(NC) for part in parts], axis=1)[None]

    out_grad = joined(top[:, :, 3 * D :])
    fc1_grad = joined(top[:, :, : 2 * D])
    fc2_grad = joined(top[:, :, 2 * D : 3 * D], fill)

    qkv_new = adamw(qkv_weight, qkv_moment, qkv_second, mix_grad, RATE_MATRIX, DECAY_MATRIX)
    out_new = adamw(
        out_weight, out_moment, out_second, out_grad, RATE_MATRIX, DECAY_MATRIX
    )
    fc1_new = adamw(
        fc1_weight, fc1_moment, fc1_second, fc1_grad, RATE_MATRIX, DECAY_MATRIX
    )
    fc2_new = adamw(
        fc2_weight, fc2_moment, fc2_second, fc2_grad, RATE_MATRIX, DECAY_MATRIX
    )
    vec_new = adamw(vectors, vector_moment, vector_second, vector_total, RATE_VECTOR, 0.0)
    return (
        block_out[None],
        input_grad[None],
        *qkv_new,
        *out_new,
        *fc1_new,
        *fc2_new,
        *vec_new,
    )


def solution(mesh):
    grid = Mesh(mesh.devices.reshape(NX, NZ, NC, NY), ("x", "z", "c", "y"))
    rows = P("y", ("x", "z", "c"), None)
    weight = P(None, ("x", "z", "c", "y"), None)
    in_specs = (rows, rows, P()) + (weight,) * 4 + (P(),) + (weight,) * 8 + (P(), P())
    out_specs = (rows, rows) + (weight,) * 12 + (P(), P(), P())
    return jax.shard_map(local, mesh=grid, in_specs=in_specs, out_specs=out_specs, check_vma=False)
```

```python
import jax
import jax.numpy as jnp
import numpy as np
from jax import lax
from jax.experimental import pallas as pl
from jax.experimental.pallas import tpu as pltpu
from jax.sharding import Mesh
from jax.sharding import PartitionSpec as P

D = 768
HEADS = 12
HD = 64
FF = 3072
LAYERS = 1
STEP = 5

EPS_NORM = 1e-05
NEGATIVE = -1e30
BETA_ONE = 0.9
BETA_TWO = 0.999
RATE_MATRIX = 0.1
RATE_VECTOR = 0.5
DECAY_MATRIX = 0.1
EPS_ADAM = 1e-08

NX = 4
NZ = 4
NC = 2
NY = 4
GH = HEADS // NX
GD = GH * HD
ROWS = 128
BLK = 64
QROWS = NX * ROWS
SEQ = 4096
NBLK = SEQ // BLK
CHUNK = 1024
GB = 4
WAYS = BLK * GB
MIX = NX * 640
BF = jnp.bfloat16
F32 = jnp.float32
VMEM = pltpu.VMEM
SMEM = pltpu.SMEM


def layer_norm(hidden, norm_gain, norm_shift):
    center = hidden - jnp.mean(hidden, axis=-1, keepdims=True)
    spread = jnp.mean(center * center, axis=-1, keepdims=True)
    return center * lax.rsqrt(spread + EPS_NORM) * norm_gain + norm_shift


def adamw(weight, moment, second, gradient, step_rate, decay_rate):
    moment_new = BETA_ONE * moment + (1.0 - BETA_ONE) * gradient
    second_new = BETA_TWO * second + (1.0 - BETA_TWO) * gradient * gradient
    moment_hat = moment_new / (1.0 - BETA_ONE**STEP)
    second_hat = second_new / (1.0 - BETA_TWO**STEP)
    weight_new = weight - step_rate * (
        moment_hat / (jnp.sqrt(second_hat) + EPS_ADAM) + decay_rate * weight
    )
    return (moment_new, second_new, weight_new)


RIGHT = [(i, (i + 1) % 4) for i in range(4)]
LEFT = [(i, (i + 3) % 4) for i in range(4)]
SWAP = [(0, 1), (1, 0)]
EVEN = [(0, 1), (1, 0), (2, 3), (3, 2)]
ODD = [(1, 2), (2, 1), (3, 0), (0, 3)]


def ring_near(part, axis):
    return lax.ppermute(part, axis, RIGHT), lax.ppermute(part, axis, LEFT)


def ring_gather(part, axis, near=None):
    half = part.shape[0] // 2
    before, after = near or ring_near(part, axis)
    far_low = lax.ppermute(before[:half], axis, RIGHT)
    far_high = lax.ppermute(after[half:], axis, LEFT)
    return jnp.concatenate([part, before, after, far_low, far_high], axis=0)


def ordered(gathered, axis):
    rows = gathered.shape[0] // 4
    me = lax.axis_index(axis)
    relative = lax.rem(4 + jnp.arange(4) - me, 4)
    slot = jnp.where(relative == 1, 2, jnp.where(relative == 2, 3, jnp.where(relative == 3, 1, 0)))
    return jnp.take(gathered.reshape(4, rows, -1), slot, axis=0).reshape(gathered.shape)


def gather_zc(part):
    own = ring_gather(part, "z")
    return own, lax.ppermute(own, "c", SWAP)


def copy_gather(part, axes):
    count = lax.axis_size(axes)
    return lax.all_to_all(jnp.broadcast_to(part[None], (count,) + part.shape), axes, 0, 0, tiled=True)


def sum_ring(value, axis):
    before, after = ring_near(value, axis)
    far = lax.ppermute(value, axis, [(i, (i + 2) % 4) for i in range(4)])
    return (value + far) + (before + after)


def widening():
    pick = np.zeros((D, 8 * 128), np.float32)
    feature = np.arange(D)
    pick[feature, feature // 6 * 8 + feature % 6] = 1.0
    return pick


def filling(part):
    pick = np.zeros((D, 8 * 128), np.float32)
    device = np.arange(128)
    pick[6 * device + part, 8 * device + 6] = 1.0
    pick[6 * device + 3 + part, 8 * device + 7] = 1.0
    return pick


def dot_nt(left, right):
    return lax.dot_general(left, right, (((1,), (1,)), ((), ())), preferred_element_type=F32)


def dot_nn(left, right):
    return lax.dot_general(left, right, (((1,), (0,)), ((), ())), preferred_element_type=F32)


def group_rows(ref, blocks, columns):
    return jnp.concatenate(
        [ref[pl.ds(pl.multiple_of(block * BLK, BLK), BLK), columns] for block in blocks], axis=0
    )


def store_group(ref, blocks, columns, value):
    for at, block in enumerate(blocks):
        rows = slice(at * BLK, (at + 1) * BLK)
        ref[pl.ds(pl.multiple_of(block * BLK, BLK), BLK), columns] = value[rows]


def group_places(blocks, shape, axis):
    index = lax.broadcasted_iota(jnp.int32, shape, axis)
    places = blocks[0] * BLK + index
    for at in range(1, len(blocks)):
        places = jnp.where(index < at * BLK, places, (blocks[at] - at) * BLK + index)
    return places


def group_of(tab, g):
    own = [tab[NBLK + GB * g + j] for j in range(GB)]
    return own, [tab[NBLK + 8 + GB * g + j] for j in range(GB)]


def sort_blocks(tab, sources, store):
    at = 0
    for source in sources:
        count = source.shape[0] // BLK

        def move(block, carry, source=source, at=at):
            place = tab[at + block]
            rows = source[pl.ds(pl.multiple_of(block * BLK, BLK), BLK), :]
            store(pl.multiple_of(place * BLK, BLK), rows)
            return carry

        lax.fori_loop(0, count, move, 0)
        at = at + count


def head_columns(head, part=0):
    return slice(part * GD + head * HD, part * GD + (head + 1) * HD)


def forward_kernel(tab, q, kv_own, kv_other, att, exact, stats, k_s, v_s):
    def store(at, rows):
        ones = jnp.ones((BLK, HD), BF)
        for head in range(GH):
            k_s[head, pl.ds(at, BLK), :] = rows[:, head_columns(head)]
            v_s[head, pl.ds(at, BLK), :] = jnp.concatenate(
                [rows[:, head_columns(head, 1)], ones], axis=1
            )

    sort_blocks(tab, (kv_own, kv_other), store)
    lane = lax.broadcasted_iota(jnp.int32, (WAYS, 128), 1)

    def group(g, carry):
        own, at_places = group_of(tab, g)
        places = group_places(at_places, (WAYS, 1), 0)
        queries = [
            group_rows(q, own, head_columns(h)) * jnp.asarray(0.125, BF)
            for h in range(GH)
        ]

        def chunk(at, state):
            start = pl.multiple_of(at * CHUNK, CHUNK)
            keys_at = start + lax.broadcasted_iota(jnp.int32, (WAYS, CHUNK), 1)
            allowed = keys_at <= places
            out = []
            for h in range(GH):
                peak, plain, extra = state[h]
                scores = dot_nt(queries[h], k_s[h, pl.ds(start, CHUNK), :])
                scores = jnp.where(allowed, scores, NEGATIVE)
                peak_new = jnp.maximum(peak, jnp.max(scores, axis=1, keepdims=True))
                shrink = jnp.exp(peak - peak_new)
                expo = jnp.exp(scores - peak_new)
                probs = expo.astype(BF)
                residue = (expo - probs.astype(F32)).astype(BF)
                values = v_s[h, pl.ds(start, CHUNK), :]
                plain = plain * shrink + dot_nn(probs, values)
                extra = extra * shrink + dot_nn(residue, values)
                out.append((peak_new, plain, extra))
            return tuple(out)

        zero = jnp.zeros((WAYS, 128), F32)
        begin = tuple((jnp.full((WAYS, 1), NEGATIVE, F32), zero, zero) for _ in range(GH))
        state = lax.fori_loop(0, lax.div(at_places[-1], CHUNK // BLK) + 1, chunk, begin)
        table = jnp.zeros((WAYS, 128), F32)
        for h in range(GH):
            peak, plain, extra = state[h]
            both = plain + extra
            mass = both[:, HD : HD + 1]
            store_group(att, own, head_columns(h), (plain[:, :HD] / mass).astype(BF))
            store_group(exact, own, head_columns(h), both[:, :HD] / mass)
            table = jnp.where(lane == h, peak + jnp.log(mass), table)
        store_group(stats, own, slice(0, 128), table)
        return carry

    lax.fori_loop(0, 8 // GB, group, 0)


def pack_kernel(back, exact, stats_in, q, packed, stats):
    lane = lax.broadcasted_iota(jnp.int32, (QROWS, 128), 1)
    table = stats_in[...]
    extra = jnp.zeros((QROWS, 128), F32)
    for h in range(GH):
        columns = head_columns(h)
        dot = jnp.sum(back[:, columns].astype(F32) * exact[:, columns], axis=1, keepdims=True)
        table = jnp.where(lane == GH + h, dot, table)
    stats[...] = table
    for j in range(2 * GH):
        value = table[:, j : j + 1]
        for t in range(3):
            piece = value.astype(BF).astype(F32)
            value = value - piece
            extra = jnp.where(lane == 3 * j + t, piece, extra)
    packed[:, :GD] = back[...]
    packed[:, GD:256] = extra[:, : 256 - GD].astype(BF)
    packed[:, 256:] = jnp.concatenate([q[...], jnp.zeros((QROWS, 256 - GD), BF)], axis=1)


def query_kernel(tab, q, back, stats, kv_own, kv_other, grad, k_s, v_s):
    def store(at, rows):
        for head in range(GH):
            k_s[head, pl.ds(at, BLK), :] = rows[:, head_columns(head)]
            v_s[head, pl.ds(at, BLK), :] = rows[:, head_columns(head, 1)]

    sort_blocks(tab, (kv_own, kv_other), store)

    def group(g, carry):
        own, at_places = group_of(tab, g)
        places = group_places(at_places, (WAYS, 1), 0)
        table = group_rows(stats, own, slice(0, 128))
        queries = [
            group_rows(q, own, head_columns(h)) * jnp.asarray(0.125, BF)
            for h in range(GH)
        ]
        backs = [group_rows(back, own, head_columns(h)) for h in range(GH)]

        def chunk(at, state):
            start = pl.multiple_of(at * CHUNK, CHUNK)
            keys_at = start + lax.broadcasted_iota(jnp.int32, (WAYS, CHUNK), 1)
            allowed = keys_at <= places
            out = []
            for h in range(GH):
                keys = k_s[h, pl.ds(start, CHUNK), :]
                scores = dot_nt(queries[h], keys) - table[:, h : h + 1]
                expo = jnp.exp(jnp.where(allowed, scores, NEGATIVE))
                dots = dot_nt(backs[h], v_s[h, pl.ds(start, CHUNK), :])
                slopes = (expo * (dots - table[:, GH + h : GH + h + 1])).astype(BF)
                out.append(state[h] + dot_nn(slopes, keys))
            return tuple(out)

        begin = tuple(jnp.zeros((WAYS, HD), F32) for _ in range(GH))
        state = lax.fori_loop(0, lax.div(at_places[-1], CHUNK // BLK) + 1, chunk, begin)
        for h in range(GH):
            store_group(grad, own, head_columns(h), (state[h] * 0.125).astype(BF))
        return carry

    lax.fori_loop(0, 8 // GB, group, 0)


def key_kernel(tab, kv, x_own, x_other, pick, grad, q_s, d_s, r_s, row_s):
    def store(at, rows):
        for head in range(GH):
            d_s[head, pl.ds(at, BLK), :] = rows[:, head_columns(head)]
            q_s[head, pl.ds(at, BLK), :] = rows[
                :, 256 + head * HD : 256 + (head + 1) * HD
            ] * jnp.asarray(0.125, BF)
        r_s[pl.ds(at, BLK), :] = rows[:, 128:256]

    sort_blocks(tab, (x_own, x_other), store)

    def rows_of(at, carry):
        start = pl.multiple_of(at * CHUNK, CHUNK)
        row_s[at] = dot_nt(pick[...], r_s[pl.ds(start, CHUNK), :])
        return carry

    lax.fori_loop(0, SEQ // CHUNK, rows_of, 0)

    def group(g, carry):
        own, at_places = group_of(tab, g)
        places = group_places(at_places, (WAYS, 1), 0)
        keys = [group_rows(kv, own, head_columns(h)) for h in range(GH)]
        values = [group_rows(kv, own, head_columns(h, 1)) for h in range(GH)]

        def chunk(at, state):
            start = pl.multiple_of(at * CHUNK, CHUNK)
            queries_at = start + lax.broadcasted_iota(jnp.int32, (WAYS, CHUNK), 1)
            allowed = places <= queries_at
            rows = row_s[at]
            out = []
            for h in range(GH):
                queries = q_s[h, pl.ds(start, CHUNK), :]
                backs = d_s[h, pl.ds(start, CHUNK), :]
                scores = dot_nt(keys[h], queries) - rows[h : h + 1, :]
                expo = jnp.exp(jnp.where(allowed, scores, NEGATIVE))
                dots = dot_nt(values[h], backs)
                slopes = (expo * (dots - rows[GH + h : GH + h + 1, :])).astype(BF)
                key_grad, value_grad = state[h]
                out.append(
                    (
                        key_grad + dot_nn(slopes, queries),
                        value_grad + dot_nn(expo.astype(BF), backs),
                    )
                )
            return tuple(out)

        zero = jnp.zeros((WAYS, HD), F32)
        begin = tuple((zero, zero) for _ in range(GH))
        state = lax.fori_loop(lax.div(at_places[0], CHUNK // BLK), SEQ // CHUNK, chunk, begin)
        for h in range(GH):
            store_group(grad, own, head_columns(h), state[h][0].astype(BF))
            store_group(grad, own, head_columns(h, 1), state[h][1].astype(BF))
        return carry

    lax.fori_loop(0, 8 // GB, group, 0)


def call(kernel, operands, outs, scratch, cost, tabled=True):
    specs = [pl.BlockSpec(memory_space=VMEM)] * (len(operands) - int(tabled))
    if tabled:
        specs = [pl.BlockSpec(memory_space=SMEM)] + specs
    return pl.pallas_call(
        kernel,
        in_specs=specs,
        out_specs=[pl.BlockSpec(memory_space=VMEM)] * len(outs),
        out_shape=[jax.ShapeDtypeStruct(shape, kind) for shape, kind in outs],
        scratch_shapes=scratch,
        compiler_params=pltpu.CompilerParams(vmem_limit_bytes=40 * 2**20),
        cost_estimate=pl.CostEstimate(flops=cost, bytes_accessed=8 * 2**20, transcendentals=0),
    )(*operands)


HEAD_SCRATCH = VMEM((GH, SEQ, HD), BF)


def attend(tab, q, kv_own, kv_other):
    return call(
        forward_kernel,
        (tab, q, kv_own, kv_other),
        [((QROWS, GD), BF), ((QROWS, GD), F32), ((QROWS, 128), F32)],
        [HEAD_SCRATCH, VMEM((GH, SEQ, 128), BF)],
        23 * 10**9,
    )


def pack(back, exact, stats, q):
    return call(
        pack_kernel,
        (back, exact, stats, q),
        [((QROWS, 512), BF), ((QROWS, 128), F32)],
        [],
        10**7,
        tabled=False,
    )


def query_grads(tab, q, back, stats, kv_own, kv_other):
    return call(
        query_kernel,
        (tab, q, back, stats, kv_own, kv_other),
        [((QROWS, GD), BF)],
        [HEAD_SCRATCH, HEAD_SCRATCH],
        18 * 10**9,
    )[0]


def key_grads(tab, kv, x_own, x_other):
    pick = np.zeros((8, 128), np.float32)
    for j in range(2 * GH):
        for t in range(3):
            pick[j, GD - 128 + 3 * j + t] = 1.0
    return call(
        key_kernel,
        (tab, kv, x_own, x_other, jnp.asarray(pick, BF)),
        [((QROWS, 2 * GD), BF)],
        [HEAD_SCRATCH, HEAD_SCRATCH, VMEM((SEQ, 128), BF), VMEM((SEQ // CHUNK, 8, CHUNK), F32)],
        24 * 10**9,
    )[0]


def block_kernel(
    att, tok, cot, vec, w, widen, block_out, grad, two, low, up, active, back_att, sums
):
    def wide(value):
        return dot_nn(value, widen[...]).astype(BF)

    def narrow(value):
        total = None
        for _ in range(3):
            piece = value.astype(BF)
            value = value - piece.astype(F32)
            part = dot_nt(piece, widen[...])
            total = part if total is None else total + part
        return total

    def row(j):
        return vec[j : j + 1, :]

    attended = jnp.concatenate([att[g] for g in range(NX)], axis=1)
    middle = tok[...].astype(F32) + dot_nn(wide(attended), w[:, :D]) + row(4)
    center = middle - jnp.mean(middle, axis=1, keepdims=True)
    inverse = lax.rsqrt(jnp.mean(center * center, axis=1, keepdims=True) + EPS_NORM)
    unit = center * inverse
    normed_two = (unit * row(5) + row(6)).astype(BF)
    two[...] = normed_two
    wide_two, wide_down = wide(normed_two), wide(cot[...])
    back_two = jnp.zeros((ROWS, 8 * 128), F32)
    down = jnp.zeros((ROWS, 8 * 128), F32)
    slope = (2.0 / np.pi) ** 0.5
    for j in range(FF // D):
        w_up = w[:, D * (1 + j) : D * (2 + j)]
        w_down = w[:, D + FF + D * j : D + FF + D * (j + 1)]
        pre = dot_nn(wide_two, w_up) + row(8 + j)
        back_active = dot_nn(wide_down, w_down)
        square = pre * pre
        bend = jnp.tanh(slope * (pre + 0.044715 * (square * pre)))
        half = 0.5 * (1.0 + bend)
        rate = half + 0.5 * pre * (1.0 - bend * bend) * (slope * (1.0 + 3 * 0.044715 * square))
        act_low = (pre * half).astype(BF)
        up_low = (back_active * rate).astype(BF)
        active[:, j * D : (j + 1) * D] = act_low
        up[:, j * D : (j + 1) * D] = up_low
        sums[4 + j : 5 + j, :] = jnp.sum(up_low.astype(F32), axis=0, keepdims=True)
        back_two = back_two + dot_nt(up_low, w_up)
        down = down + dot_nt(act_low, w_down)
    back_two = narrow(back_two)
    back_unit = back_two * row(5)
    back_middle = inverse * (
        back_unit
        - jnp.mean(back_unit, axis=1, keepdims=True)
        - unit * jnp.mean(back_unit * unit, axis=1, keepdims=True)
    )
    gradient = cot[...].astype(F32) + back_middle
    grad[...] = gradient
    branch_low = gradient.astype(BF)
    low[...] = branch_low
    back = dot_nt(dot_nt(branch_low, w[:, :D]).astype(BF), widen[...]).astype(BF)
    for g in range(NX):
        back_att[g] = back[:, g * GD : (g + 1) * GD]
    block_out[...] = middle + narrow(down) + row(7)
    sums[0:1, :] = jnp.sum(branch_low.astype(F32), axis=0, keepdims=True)
    sums[1:2, :] = jnp.sum(back_two * unit, axis=0, keepdims=True)
    sums[2:3, :] = jnp.sum(back_two, axis=0, keepdims=True)
    sums[3:4, :] = jnp.sum(cot[...].astype(F32), axis=0, keepdims=True)


def feed_forward(*operands):
    return call(
        block_kernel,
        operands,
        [
            ((ROWS, D), F32),
            ((ROWS, D), F32),
            ((ROWS, D), BF),
            ((ROWS, D), BF),
            ((ROWS, FF), BF),
            ((ROWS, FF), BF),
            ((NX, ROWS, GD), BF),
            ((8, D), F32),
        ],
        [],
        20 * 10**9,
        tabled=False,
    )


def rest_kernel(att, two, down, branch, up, active, spread_t, fill_t, grad):
    def across(table, value):
        return dot_nt(table, value).astype(BF)

    two_t, down_t = across(spread_t[...], two[...]), across(spread_t[...], down[...])
    att_t = across(spread_t[...], att[...])
    last = active[:, D:]
    tops = ((two_t, up[:, :D]), (two_t, up[:, D:]), (down_t, active[:, :D]))
    for j, (left, right) in enumerate(tops):
        left = jnp.concatenate([left, across(fill_t[j], down[...])], axis=1)
        right = jnp.concatenate([right, last], axis=0)
        grad[:, j * D : (j + 1) * D] = dot_nn(left, right).astype(BF)
    grad[:, 3 * D :] = dot_nn(att_t, branch[...]).astype(BF)


def rest_grads(*rows):
    fills = np.stack([filling(j).T for j in range(3)])
    return call(
        rest_kernel,
        (*rows, jnp.asarray(widening().T, BF), jnp.asarray(fills, BF)),
        [((8 * 128, 7 * (D // 2)), BF)],
        [],
        9 * 10**9,
        tabled=False,
    )[0]


def joint_kernel(wide_t, back_q, back_kv, rest, joint):
    right = jnp.concatenate([back_q[...], back_kv[...]], axis=1)
    rows, size = joint.shape[0], MIX // NX
    blank = jnp.zeros((rows, size - 3 * GD), BF)
    for x in range(NX):
        part = dot_nn(wide_t[x * rows : (x + 1) * rows, :], right).astype(BF)
        joint[:, x * size : (x + 1) * size] = jnp.concatenate([part, blank], axis=1)
    joint[:, MIX:] = rest[...]


def joint_grads(*operands):
    return call(
        joint_kernel,
        operands,
        [((256, MIX + 7 * (D // 2)), BF)],
        [],
        3 * 10**9,
        tabled=False,
    )[0]


def place_table(pair_of_device):
    z, core = lax.axis_index("z"), lax.axis_index("c")
    pairs = pair_of_device.reshape(NX, NZ, NC).transpose(1, 2, 0)
    order = jnp.stack([z, (z + 3) % 4, (z + 1) % 4, (z + 2) % 4])
    pairs = jnp.take(pairs, order, axis=0)
    pairs = jnp.stack([jnp.take(pairs, core, axis=1), jnp.take(pairs, 1 - core, axis=1)])
    blocks = jnp.stack([pairs, NBLK - 1 - pairs], axis=-1).reshape(NBLK)
    own = blocks[: 2 * NX]
    rank = jnp.sum(own[:, None] > own[None, :], axis=1)
    hit = rank[None, :] == jnp.arange(2 * NX)[:, None]
    index = jnp.sum(jnp.where(hit, jnp.arange(2 * NX)[None, :], 0), axis=1)
    place = jnp.sum(jnp.where(hit, own[None, :], 0), axis=1)
    return jnp.concatenate([blocks, index, place]).astype(jnp.int32)


def local(
    tokens,
    cotangent,
    pair_of_device,
    qkv_weight,
    out_weight,
    fc1_weight,
    fc2_weight,
    vectors,
    qkv_moment,
    qkv_second,
    out_moment,
    out_second,
    fc1_moment,
    fc1_second,
    fc2_moment,
    fc2_second,
    vector_moment,
    vector_second,
):
    xi, core = lax.axis_index("x"), lax.axis_index("c")
    everyone = ("x", "z", "c", "y")
    vector = vectors[0]
    tab = place_table(pair_of_device)
    widen = jnp.asarray(widening(), BF)

    mix = qkv_weight[0].astype(BF).reshape(6, 3, NX, GD).transpose(2, 0, 1, 3).reshape(NX, 1, 6, 3 * GD)
    mix = jnp.broadcast_to(mix, (NX, NY, 6, 3 * GD)).reshape(NX * NY, 6, 3 * GD)
    mix = lax.all_to_all(mix, ("x", "y"), 0, 0, tiled=True)
    mix = copy_gather(mix.reshape(NX * NY * 6, 3 * GD), ("z", "c"))
    mix = mix.reshape(NZ, NC, NX, NY, 6, 3 * GD).transpose(2, 0, 1, 3, 4, 5)
    tokens4 = ordered(ring_gather(tokens[0], "x"), "x")

    rest = jnp.concatenate([p[0].astype(BF) for p in (out_weight, fc1_weight, fc2_weight)], axis=1)
    rest = jnp.pad(rest, ((0, 2), (0, 0)))[None]
    rest, mix, tokens4 = lax.optimization_barrier((rest, mix, tokens4))
    rest_all = lax.all_gather(rest, everyone, axis=0, tiled=True).reshape(8 * 128, D + 2 * FF)

    w_mix = mix.reshape(D, 3 * GD)

    hidden4 = tokens4.astype(F32)
    normed4 = layer_norm(hidden4, vector[0], vector[1]).astype(BF)
    projected = jnp.dot(normed4, w_mix, preferred_element_type=F32)
    group_bias = lax.dynamic_slice_in_dim(vector[2:4], xi * GD, GD, 1)
    q4 = (projected[:, :GD] + group_bias[0]).astype(BF)
    k4 = projected[:, GD : 2 * GD].astype(BF)
    v4 = (projected[:, 2 * GD :] + group_bias[1]).astype(BF)
    kv4 = jnp.concatenate([k4, v4], axis=1)
    wide4 = lax.dot_general(
        widen, normed4, (((0,), (1,)), ((), ())), preferred_element_type=F32
    ).astype(BF)
    kv_own, kv_other = gather_zc(kv4)
    q4, wide4 = lax.optimization_barrier((q4, wide4))
    att4, exact4, stats4 = attend(tab, q4, kv_own, kv_other)
    attended = lax.all_to_all(att4.reshape(NX, ROWS, GD), "x", 0, 0, tiled=True)
    block_out, gradient, normed_two, branch_low, up_low, active, back_attended, early_rows = (
        feed_forward(attended, tokens[0], cotangent[0], vector, rest_all, widen)
    )
    attended = attended.transpose(1, 0, 2).reshape(ROWS, D)
    down_low = cotangent[0]
    back4 = lax.all_to_all(back_attended, "x", 0, 0, tiled=True).reshape(QROWS, GD)
    packed, stats_all = pack(back4, exact4, stats4, q4)
    x_near = ring_near(packed, "z")

    late = (attended, normed_two, down_low, branch_low, up_low, active)

    def outer(left, right):
        return jnp.einsum("rc,re->ce", left, right, preferred_element_type=F32).astype(BF)

    def half_of(value, which):
        size = value.shape[1] // 2
        return lax.dynamic_slice_in_dim(value, which * size, size, 1)

    mine = list(late[:3]) + [half_of(v, core) for v in late[3:]]
    theirs = list(late[:3]) + [half_of(v, 1 - core) for v in late[3:]]
    got = lax.ppermute(jnp.concatenate(theirs, axis=1), "c", SWAP)
    at, both = 0, []
    for value in mine:
        both.append(jnp.concatenate([value, got[:, at : at + value.shape[1]]], axis=0))
        at = at + value.shape[1]
    both, packed = lax.optimization_barrier((both, packed))
    rest_grad, back_in = lax.optimization_barrier((rest_grads(*both), back4))
    rest_grad = lax.psum_scatter(rest_grad, "x", scatter_dimension=0, tiled=True)

    back_q4 = query_grads(tab, q4, back_in, stats_all, kv_own, kv_other)
    back_q4, x_near = lax.optimization_barrier((back_q4, x_near))
    x_own = ring_gather(packed, "z", x_near)
    x_other = lax.ppermute(x_own, "c", SWAP)
    back_kv4 = key_grads(tab, kv4, x_own, x_other)
    mixed4 = jnp.concatenate([back_q4, back_kv4], axis=1)

    joint = joint_grads(wide4, back_q4, back_kv4, rest_grad).reshape(32, 8, MIX + 7 * (D // 2))
    joint = lax.all_to_all(joint, ("z", "c", "y"), 0, 0, tiled=True)
    back_normed4 = dot_nt(mixed4, w_mix)
    _, shift_back = jax.vjp(
        lambda gain, shift: layer_norm(hidden4, gain, shift), vector[0], vector[1]
    )
    gain_one, shift_one = shift_back(back_normed4)
    pieces = back_normed4.astype(BF)

    def piece_of(device):
        return lax.dynamic_slice_in_dim(pieces, lax.rem(device, NX) * ROWS, ROWS, 0)

    back_normed = lax.dynamic_slice_in_dim(back_normed4, xi * ROWS, ROWS, 0)
    for step in (1, 2, 3):
        moved = lax.ppermute(piece_of(xi + step), "x", [(i, (i + step) % 4) for i in range(4)])
        back_normed = back_normed + moved.astype(F32)

    def column_sum(value):
        return jnp.sum(value.astype(F32), axis=0)

    def at_group(value):
        return lax.dynamic_update_slice_in_dim(jnp.zeros((D,), F32), value, xi * GD, 0)

    late_rows = jnp.stack(
        [
            gain_one,
            shift_one,
            at_group(column_sum(back_q4)),
            at_group(column_sum(back_kv4[:, GD:])),
        ]
    )
    vector_part = jnp.concatenate([late_rows, early_rows], axis=0)
    vector_part = vector_part + lax.ppermute(vector_part, "c", SWAP)
    vector_part = sum_ring(vector_part, "y")
    joint, vector_part = lax.optimization_barrier((joint, vector_part))
    vector_total = sum_ring(sum_ring(vector_part, "z"), "x")[None]

    hidden = tokens[0].astype(F32)
    _, first_back = jax.vjp(lambda h: layer_norm(h, vector[0], vector[1]), hidden)
    input_grad = gradient + first_back(back_normed)[0]

    mix_grad = jnp.sum(joint[:, :, :MIX].astype(F32), axis=0).astype(BF)
    mix_grad = lax.all_to_all(
        mix_grad.reshape(8, NX, MIX // NX).transpose(1, 0, 2), "x", 0, 0, tiled=True
    )[:, :6, : 3 * GD].astype(F32)
    mix_grad = (
        mix_grad.reshape(NX, 6, 3, GD).transpose(1, 2, 0, 3).reshape(1, 6, 3 * D)
    )
    wide_sum = jnp.sum(
        joint[:, :, MIX:].reshape(NZ, NC, NY, 8, 7 * (D // 2)).astype(F32), axis=(0, 2)
    )
    top, fill = wide_sum[:, :6], wide_sum[:, 6:, : 3 * D].reshape(NC, 6, D)

    def joined(*parts):
        return jnp.concatenate([part[j] for j in range(NC) for part in parts], axis=1)[None]

    out_grad = joined(top[:, :, 3 * D :])
    fc1_grad = joined(top[:, :, : 2 * D])
    fc2_grad = joined(top[:, :, 2 * D : 3 * D], fill)

    qkv_new = adamw(qkv_weight, qkv_moment, qkv_second, mix_grad, RATE_MATRIX, DECAY_MATRIX)
    out_new = adamw(
        out_weight, out_moment, out_second, out_grad, RATE_MATRIX, DECAY_MATRIX
    )
    fc1_new = adamw(
        fc1_weight, fc1_moment, fc1_second, fc1_grad, RATE_MATRIX, DECAY_MATRIX
    )
    fc2_new = adamw(
        fc2_weight, fc2_moment, fc2_second, fc2_grad, RATE_MATRIX, DECAY_MATRIX
    )
    vec_new = adamw(vectors, vector_moment, vector_second, vector_total, RATE_VECTOR, 0.0)
    return (
        block_out[None],
        input_grad[None],
        *qkv_new,
        *out_new,
        *fc1_new,
        *fc2_new,
        *vec_new,
    )


def solution(mesh):
    grid = Mesh(mesh.devices.reshape(NX, NZ, NC, NY), ("x", "z", "c", "y"))
    rows = P("y", ("x", "z", "c"), None)
    weight = P(None, ("x", "z", "c", "y"), None)
    in_specs = (rows, rows, P()) + (weight,) * 4 + (P(),) + (weight,) * 8 + (P(), P())
    out_specs = (rows, rows) + (weight,) * 12 + (P(), P(), P())
    return jax.shard_map(local, mesh=grid, in_specs=in_specs, out_specs=out_specs, check_vma=False)
```

```python
import jax
import jax.numpy as jnp
import numpy as np
from jax import lax
from jax.experimental import pallas as pl
from jax.experimental.pallas import tpu as pltpu
from jax.sharding import Mesh
from jax.sharding import PartitionSpec as P

D = 768
HEADS = 12
HD = 64
FF = 3072
LAYERS = 1
STEP = 5

EPS_NORM = 1e-05
NEGATIVE = -1e30
BETA_ONE = 0.9
BETA_TWO = 0.999
RATE_MATRIX = 0.1
RATE_VECTOR = 0.5
DECAY_MATRIX = 0.1
EPS_ADAM = 1e-08

NX = 4
NZ = 4
NC = 2
NY = 4
GH = HEADS // NX
GD = GH * HD
ROWS = 128
BLK = 64
QROWS = NX * ROWS
SEQ = 4096
NBLK = SEQ // BLK
CHUNK = 2048
GB = 4
WAYS = BLK * GB
MIX = NX * 640
BF = jnp.bfloat16
F32 = jnp.float32
VMEM = pltpu.VMEM
SMEM = pltpu.SMEM


def layer_norm(hidden, norm_gain, norm_shift):
    center = hidden - jnp.mean(hidden, axis=-1, keepdims=True)
    spread = jnp.mean(center * center, axis=-1, keepdims=True)
    return center * lax.rsqrt(spread + EPS_NORM) * norm_gain + norm_shift


def adamw(weight, moment, second, gradient, step_rate, decay_rate):
    moment_new = BETA_ONE * moment + (1.0 - BETA_ONE) * gradient
    second_new = BETA_TWO * second + (1.0 - BETA_TWO) * gradient * gradient
    moment_hat = moment_new / (1.0 - BETA_ONE**STEP)
    second_hat = second_new / (1.0 - BETA_TWO**STEP)
    weight_new = weight - step_rate * (
        moment_hat / (jnp.sqrt(second_hat) + EPS_ADAM) + decay_rate * weight
    )
    return (moment_new, second_new, weight_new)


RIGHT = [(i, (i + 1) % 4) for i in range(4)]
LEFT = [(i, (i + 3) % 4) for i in range(4)]
SWAP = [(0, 1), (1, 0)]
EVEN = [(0, 1), (1, 0), (2, 3), (3, 2)]
ODD = [(1, 2), (2, 1), (3, 0), (0, 3)]


def ring_near(part, axis):
    return lax.ppermute(part, axis, RIGHT), lax.ppermute(part, axis, LEFT)


def ring_gather(part, axis, near=None):
    half = part.shape[0] // 2
    before, after = near or ring_near(part, axis)
    far_low = lax.ppermute(before[:half], axis, RIGHT)
    far_high = lax.ppermute(after[half:], axis, LEFT)
    return jnp.concatenate([part, before, after, far_low, far_high], axis=0)


def ordered(gathered, axis):
    rows = gathered.shape[0] // 4
    me = lax.axis_index(axis)
    relative = lax.rem(4 + jnp.arange(4) - me, 4)
    slot = jnp.where(relative == 1, 2, jnp.where(relative == 2, 3, jnp.where(relative == 3, 1, 0)))
    return jnp.take(gathered.reshape(4, rows, -1), slot, axis=0).reshape(gathered.shape)


def gather_zc(part):
    own = ring_gather(part, "z")
    return own, lax.ppermute(own, "c", SWAP)


def copy_gather(part, axes):
    count = lax.axis_size(axes)
    return lax.all_to_all(jnp.broadcast_to(part[None], (count,) + part.shape), axes, 0, 0, tiled=True)


def sum_ring(value, axis):
    before, after = ring_near(value, axis)
    far = lax.ppermute(value, axis, [(i, (i + 2) % 4) for i in range(4)])
    return (value + far) + (before + after)


def widening():
    pick = np.zeros((D, 8 * 128), np.float32)
    feature = np.arange(D)
    pick[feature, feature // 6 * 8 + feature % 6] = 1.0
    return pick


def filling(part):
    pick = np.zeros((D, 8 * 128), np.float32)
    device = np.arange(128)
    pick[6 * device + part, 8 * device + 6] = 1.0
    pick[6 * device + 3 + part, 8 * device + 7] = 1.0
    return pick


def dot_nt(left, right):
    return lax.dot_general(left, right, (((1,), (1,)), ((), ())), preferred_element_type=F32)


def dot_nn(left, right):
    return lax.dot_general(left, right, (((1,), (0,)), ((), ())), preferred_element_type=F32)


def group_rows(ref, blocks, columns):
    return jnp.concatenate(
        [ref[pl.ds(pl.multiple_of(block * BLK, BLK), BLK), columns] for block in blocks], axis=0
    )


def store_group(ref, blocks, columns, value):
    for at, block in enumerate(blocks):
        rows = slice(at * BLK, (at + 1) * BLK)
        ref[pl.ds(pl.multiple_of(block * BLK, BLK), BLK), columns] = value[rows]


def group_places(blocks, shape, axis):
    index = lax.broadcasted_iota(jnp.int32, shape, axis)
    places = blocks[0] * BLK + index
    for at in range(1, len(blocks)):
        places = jnp.where(index < at * BLK, places, (blocks[at] - at) * BLK + index)
    return places


def group_of(tab, g):
    own = [tab[NBLK + GB * g + j] for j in range(GB)]
    return own, [tab[NBLK + 8 + GB * g + j] for j in range(GB)]


def sort_blocks(tab, sources, store):
    at = 0
    for source in sources:
        count = source.shape[0] // BLK

        def move(block, carry, source=source, at=at):
            place = tab[at + block]
            rows = source[pl.ds(pl.multiple_of(block * BLK, BLK), BLK), :]
            store(pl.multiple_of(place * BLK, BLK), rows)
            return carry

        lax.fori_loop(0, count, move, 0)
        at = at + count


def head_columns(head, part=0):
    return slice(part * GD + head * HD, part * GD + (head + 1) * HD)


def forward_kernel(tab, q, kv_own, kv_other, att, exact, stats, k_s, v_s):
    def store(at, rows):
        ones = jnp.ones((BLK, HD), BF)
        for head in range(GH):
            k_s[head, pl.ds(at, BLK), :] = rows[:, head_columns(head)]
            v_s[head, pl.ds(at, BLK), :] = jnp.concatenate(
                [rows[:, head_columns(head, 1)], ones], axis=1
            )

    sort_blocks(tab, (kv_own, kv_other), store)
    lane = lax.broadcasted_iota(jnp.int32, (WAYS, 128), 1)

    def group(g, carry):
        own, at_places = group_of(tab, g)
        places = group_places(at_places, (WAYS, 1), 0)
        queries = [
            group_rows(q, own, head_columns(h)) * jnp.asarray(0.125, BF)
            for h in range(GH)
        ]

        def chunk(at, state):
            start = pl.multiple_of(at * CHUNK, CHUNK)
            keys_at = start + lax.broadcasted_iota(jnp.int32, (WAYS, CHUNK), 1)
            allowed = keys_at <= places
            out = []
            for h in range(GH):
                peak, plain, extra = state[h]
                scores = dot_nt(queries[h], k_s[h, pl.ds(start, CHUNK), :])
                scores = jnp.where(allowed, scores, NEGATIVE)
                peak_new = jnp.maximum(peak, jnp.max(scores, axis=1, keepdims=True))
                shrink = jnp.exp(peak - peak_new)
                expo = jnp.exp(scores - peak_new)
                probs = expo.astype(BF)
                residue = (expo - probs.astype(F32)).astype(BF)
                values = v_s[h, pl.ds(start, CHUNK), :]
                plain = plain * shrink + dot_nn(probs, values)
                extra = extra * shrink + dot_nn(residue, values)
                out.append((peak_new, plain, extra))
            return tuple(out)

        zero = jnp.zeros((WAYS, 128), F32)
        begin = tuple((jnp.full((WAYS, 1), NEGATIVE, F32), zero, zero) for _ in range(GH))
        state = lax.fori_loop(0, lax.div(at_places[-1], CHUNK // BLK) + 1, chunk, begin)
        table = jnp.zeros((WAYS, 128), F32)
        for h in range(GH):
            peak, plain, extra = state[h]
            both = plain + extra
            mass = both[:, HD : HD + 1]
            store_group(att, own, head_columns(h), (plain[:, :HD] / mass).astype(BF))
            store_group(exact, own, head_columns(h), both[:, :HD] / mass)
            table = jnp.where(lane == h, peak + jnp.log(mass), table)
        store_group(stats, own, slice(0, 128), table)
        return carry

    lax.fori_loop(0, 8 // GB, group, 0)


def pack_kernel(back, exact, stats_in, q, packed, stats):
    lane = lax.broadcasted_iota(jnp.int32, (QROWS, 128), 1)
    table = stats_in[...]
    extra = jnp.zeros((QROWS, 128), F32)
    for h in range(GH):
        columns = head_columns(h)
        dot = jnp.sum(back[:, columns].astype(F32) * exact[:, columns], axis=1, keepdims=True)
        table = jnp.where(lane == GH + h, dot, table)
    stats[...] = table
    for j in range(2 * GH):
        value = table[:, j : j + 1]
        for t in range(3):
            piece = value.astype(BF).astype(F32)
            value = value - piece
            extra = jnp.where(lane == 3 * j + t, piece, extra)
    packed[:, :GD] = back[...]
    packed[:, GD:256] = extra[:, : 256 - GD].astype(BF)
    packed[:, 256:] = jnp.concatenate([q[...], jnp.zeros((QROWS, 256 - GD), BF)], axis=1)


def query_kernel(tab, q, back, stats, kv_own, kv_other, grad, k_s, v_s):
    def store(at, rows):
        for head in range(GH):
            k_s[head, pl.ds(at, BLK), :] = rows[:, head_columns(head)]
            v_s[head, pl.ds(at, BLK), :] = rows[:, head_columns(head, 1)]

    sort_blocks(tab, (kv_own, kv_other), store)

    def group(g, carry):
        own, at_places = group_of(tab, g)
        places = group_places(at_places, (WAYS, 1), 0)
        table = group_rows(stats, own, slice(0, 128))
        queries = [
            group_rows(q, own, head_columns(h)) * jnp.asarray(0.125, BF)
            for h in range(GH)
        ]
        backs = [group_rows(back, own, head_columns(h)) for h in range(GH)]

        def chunk(at, state):
            start = pl.multiple_of(at * CHUNK, CHUNK)
            keys_at = start + lax.broadcasted_iota(jnp.int32, (WAYS, CHUNK), 1)
            allowed = keys_at <= places
            out = []
            for h in range(GH):
                keys = k_s[h, pl.ds(start, CHUNK), :]
                scores = dot_nt(queries[h], keys) - table[:, h : h + 1]
                expo = jnp.exp(jnp.where(allowed, scores, NEGATIVE))
                dots = dot_nt(backs[h], v_s[h, pl.ds(start, CHUNK), :])
                slopes = (expo * (dots - table[:, GH + h : GH + h + 1])).astype(BF)
                out.append(state[h] + dot_nn(slopes, keys))
            return tuple(out)

        begin = tuple(jnp.zeros((WAYS, HD), F32) for _ in range(GH))
        state = lax.fori_loop(0, lax.div(at_places[-1], CHUNK // BLK) + 1, chunk, begin)
        for h in range(GH):
            store_group(grad, own, head_columns(h), (state[h] * 0.125).astype(BF))
        return carry

    lax.fori_loop(0, 8 // GB, group, 0)


def key_kernel(tab, kv, x_own, x_other, pick, grad, q_s, d_s, r_s, row_s):
    def store(at, rows):
        for head in range(GH):
            d_s[head, pl.ds(at, BLK), :] = rows[:, head_columns(head)]
            q_s[head, pl.ds(at, BLK), :] = rows[
                :, 256 + head * HD : 256 + (head + 1) * HD
            ] * jnp.asarray(0.125, BF)
        r_s[pl.ds(at, BLK), :] = rows[:, 128:256]

    sort_blocks(tab, (x_own, x_other), store)

    def rows_of(at, carry):
        start = pl.multiple_of(at * CHUNK, CHUNK)
        row_s[at] = dot_nt(pick[...], r_s[pl.ds(start, CHUNK), :])
        return carry

    lax.fori_loop(0, SEQ // CHUNK, rows_of, 0)

    def group(g, carry):
        own, at_places = group_of(tab, g)
        places = group_places(at_places, (WAYS, 1), 0)
        keys = [group_rows(kv, own, head_columns(h)) for h in range(GH)]
        values = [group_rows(kv, own, head_columns(h, 1)) for h in range(GH)]

        def chunk(at, state):
            start = pl.multiple_of(at * CHUNK, CHUNK)
            queries_at = start + lax.broadcasted_iota(jnp.int32, (WAYS, CHUNK), 1)
            allowed = places <= queries_at
            rows = row_s[at]
            out = []
            for h in range(GH):
                queries = q_s[h, pl.ds(start, CHUNK), :]
                backs = d_s[h, pl.ds(start, CHUNK), :]
                scores = dot_nt(keys[h], queries) - rows[h : h + 1, :]
                expo = jnp.exp(jnp.where(allowed, scores, NEGATIVE))
                dots = dot_nt(values[h], backs)
                slopes = (expo * (dots - rows[GH + h : GH + h + 1, :])).astype(BF)
                key_grad, value_grad = state[h]
                out.append(
                    (
                        key_grad + dot_nn(slopes, queries),
                        value_grad + dot_nn(expo.astype(BF), backs),
                    )
                )
            return tuple(out)

        zero = jnp.zeros((WAYS, HD), F32)
        begin = tuple((zero, zero) for _ in range(GH))
        state = lax.fori_loop(lax.div(at_places[0], CHUNK // BLK), SEQ // CHUNK, chunk, begin)
        for h in range(GH):
            store_group(grad, own, head_columns(h), state[h][0].astype(BF))
            store_group(grad, own, head_columns(h, 1), state[h][1].astype(BF))
        return carry

    lax.fori_loop(0, 8 // GB, group, 0)


def call(kernel, operands, outs, scratch, cost, tabled=True):
    specs = [pl.BlockSpec(memory_space=VMEM)] * (len(operands) - int(tabled))
    if tabled:
        specs = [pl.BlockSpec(memory_space=SMEM)] + specs
    return pl.pallas_call(
        kernel,
        in_specs=specs,
        out_specs=[pl.BlockSpec(memory_space=VMEM)] * len(outs),
        out_shape=[jax.ShapeDtypeStruct(shape, kind) for shape, kind in outs],
        scratch_shapes=scratch,
        compiler_params=pltpu.CompilerParams(vmem_limit_bytes=40 * 2**20),
        cost_estimate=pl.CostEstimate(flops=cost, bytes_accessed=8 * 2**20, transcendentals=0),
    )(*operands)


HEAD_SCRATCH = VMEM((GH, SEQ, HD), BF)


def attend(tab, q, kv_own, kv_other):
    return call(
        forward_kernel,
        (tab, q, kv_own, kv_other),
        [((QROWS, GD), BF), ((QROWS, GD), F32), ((QROWS, 128), F32)],
        [HEAD_SCRATCH, VMEM((GH, SEQ, 128), BF)],
        23 * 10**9,
    )


def pack(back, exact, stats, q):
    return call(
        pack_kernel,
        (back, exact, stats, q),
        [((QROWS, 512), BF), ((QROWS, 128), F32)],
        [],
        10**7,
        tabled=False,
    )


def query_grads(tab, q, back, stats, kv_own, kv_other):
    return call(
        query_kernel,
        (tab, q, back, stats, kv_own, kv_other),
        [((QROWS, GD), BF)],
        [HEAD_SCRATCH, HEAD_SCRATCH],
        18 * 10**9,
    )[0]


def key_grads(tab, kv, x_own, x_other):
    pick = np.zeros((8, 128), np.float32)
    for j in range(2 * GH):
        for t in range(3):
            pick[j, GD - 128 + 3 * j + t] = 1.0
    return call(
        key_kernel,
        (tab, kv, x_own, x_other, jnp.asarray(pick, BF)),
        [((QROWS, 2 * GD), BF)],
        [HEAD_SCRATCH, HEAD_SCRATCH, VMEM((SEQ, 128), BF), VMEM((SEQ // CHUNK, 8, CHUNK), F32)],
        24 * 10**9,
    )[0]


def block_kernel(
    att, tok, cot, vec, w, widen, block_out, grad, two, low, up, active, back_att, sums
):
    def wide(value):
        return dot_nn(value, widen[...]).astype(BF)

    def narrow(value):
        total = None
        for _ in range(3):
            piece = value.astype(BF)
            value = value - piece.astype(F32)
            part = dot_nt(piece, widen[...])
            total = part if total is None else total + part
        return total

    def row(j):
        return vec[j : j + 1, :]

    attended = jnp.concatenate([att[g] for g in range(NX)], axis=1)
    middle = tok[...].astype(F32) + dot_nn(wide(attended), w[:, :D]) + row(4)
    center = middle - jnp.mean(middle, axis=1, keepdims=True)
    inverse = lax.rsqrt(jnp.mean(center * center, axis=1, keepdims=True) + EPS_NORM)
    unit = center * inverse
    normed_two = (unit * row(5) + row(6)).astype(BF)
    two[...] = normed_two
    wide_two, wide_down = wide(normed_two), wide(cot[...])
    back_two = jnp.zeros((ROWS, 8 * 128), F32)
    down = jnp.zeros((ROWS, 8 * 128), F32)
    slope = (2.0 / np.pi) ** 0.5
    for j in range(FF // D):
        w_up = w[:, D * (1 + j) : D * (2 + j)]
        w_down = w[:, D + FF + D * j : D + FF + D * (j + 1)]
        pre = dot_nn(wide_two, w_up) + row(8 + j)
        back_active = dot_nn(wide_down, w_down)
        square = pre * pre
        bend = jnp.tanh(slope * (pre + 0.044715 * (square * pre)))
        half = 0.5 * (1.0 + bend)
        rate = half + 0.5 * pre * (1.0 - bend * bend) * (slope * (1.0 + 3 * 0.044715 * square))
        act_low = (pre * half).astype(BF)
        up_low = (back_active * rate).astype(BF)
        active[:, j * D : (j + 1) * D] = act_low
        up[:, j * D : (j + 1) * D] = up_low
        sums[4 + j : 5 + j, :] = jnp.sum(up_low.astype(F32), axis=0, keepdims=True)
        back_two = back_two + dot_nt(up_low, w_up)
        down = down + dot_nt(act_low, w_down)
    back_two = narrow(back_two)
    back_unit = back_two * row(5)
    back_middle = inverse * (
        back_unit
        - jnp.mean(back_unit, axis=1, keepdims=True)
        - unit * jnp.mean(back_unit * unit, axis=1, keepdims=True)
    )
    gradient = cot[...].astype(F32) + back_middle
    grad[...] = gradient
    branch_low = gradient.astype(BF)
    low[...] = branch_low
    back = dot_nt(dot_nt(branch_low, w[:, :D]).astype(BF), widen[...]).astype(BF)
    for g in range(NX):
        back_att[g] = back[:, g * GD : (g + 1) * GD]
    block_out[...] = middle + narrow(down) + row(7)
    sums[0:1, :] = jnp.sum(branch_low.astype(F32), axis=0, keepdims=True)
    sums[1:2, :] = jnp.sum(back_two * unit, axis=0, keepdims=True)
    sums[2:3, :] = jnp.sum(back_two, axis=0, keepdims=True)
    sums[3:4, :] = jnp.sum(cot[...].astype(F32), axis=0, keepdims=True)


def feed_forward(*operands):
    return call(
        block_kernel,
        operands,
        [
            ((ROWS, D), F32),
            ((ROWS, D), F32),
            ((ROWS, D), BF),
            ((ROWS, D), BF),
            ((ROWS, FF), BF),
            ((ROWS, FF), BF),
            ((NX, ROWS, GD), BF),
            ((8, D), F32),
        ],
        [],
        20 * 10**9,
        tabled=False,
    )


def rest_kernel(att, two, down, branch, up, active, spread_t, fill_t, grad):
    def across(table, value):
        return dot_nt(table, value).astype(BF)

    two_t, down_t = across(spread_t[...], two[...]), across(spread_t[...], down[...])
    att_t = across(spread_t[...], att[...])
    last = active[:, D:]
    tops = ((two_t, up[:, :D]), (two_t, up[:, D:]), (down_t, active[:, :D]))
    for j, (left, right) in enumerate(tops):
        left = jnp.concatenate([left, across(fill_t[j], down[...])], axis=1)
        right = jnp.concatenate([right, last], axis=0)
        grad[:, j * D : (j + 1) * D] = dot_nn(left, right).astype(BF)
    grad[:, 3 * D :] = dot_nn(att_t, branch[...]).astype(BF)


def rest_grads(*rows):
    fills = np.stack([filling(j).T for j in range(3)])
    return call(
        rest_kernel,
        (*rows, jnp.asarray(widening().T, BF), jnp.asarray(fills, BF)),
        [((8 * 128, 7 * (D // 2)), BF)],
        [],
        9 * 10**9,
        tabled=False,
    )[0]


def joint_kernel(wide_t, back_q, back_kv, rest, joint):
    right = jnp.concatenate([back_q[...], back_kv[...]], axis=1)
    rows, size = joint.shape[0], MIX // NX
    blank = jnp.zeros((rows, size - 3 * GD), BF)
    for x in range(NX):
        part = dot_nn(wide_t[x * rows : (x + 1) * rows, :], right).astype(BF)
        joint[:, x * size : (x + 1) * size] = jnp.concatenate([part, blank], axis=1)
    joint[:, MIX:] = rest[...]


def joint_grads(*operands):
    return call(
        joint_kernel,
        operands,
        [((256, MIX + 7 * (D // 2)), BF)],
        [],
        3 * 10**9,
        tabled=False,
    )[0]


def place_table(pair_of_device):
    z, core = lax.axis_index("z"), lax.axis_index("c")
    pairs = pair_of_device.reshape(NX, NZ, NC).transpose(1, 2, 0)
    order = jnp.stack([z, (z + 3) % 4, (z + 1) % 4, (z + 2) % 4])
    pairs = jnp.take(pairs, order, axis=0)
    pairs = jnp.stack([jnp.take(pairs, core, axis=1), jnp.take(pairs, 1 - core, axis=1)])
    blocks = jnp.stack([pairs, NBLK - 1 - pairs], axis=-1).reshape(NBLK)
    own = blocks[: 2 * NX]
    rank = jnp.sum(own[:, None] > own[None, :], axis=1)
    hit = rank[None, :] == jnp.arange(2 * NX)[:, None]
    index = jnp.sum(jnp.where(hit, jnp.arange(2 * NX)[None, :], 0), axis=1)
    place = jnp.sum(jnp.where(hit, own[None, :], 0), axis=1)
    return jnp.concatenate([blocks, index, place]).astype(jnp.int32)


def local(
    tokens,
    cotangent,
    pair_of_device,
    qkv_weight,
    out_weight,
    fc1_weight,
    fc2_weight,
    vectors,
    qkv_moment,
    qkv_second,
    out_moment,
    out_second,
    fc1_moment,
    fc1_second,
    fc2_moment,
    fc2_second,
    vector_moment,
    vector_second,
):
    xi, core = lax.axis_index("x"), lax.axis_index("c")
    everyone = ("x", "z", "c", "y")
    vector = vectors[0]
    tab = place_table(pair_of_device)
    widen = jnp.asarray(widening(), BF)

    mix = qkv_weight[0].astype(BF).reshape(6, 3, NX, GD).transpose(2, 0, 1, 3).reshape(NX, 1, 6, 3 * GD)
    mix = jnp.broadcast_to(mix, (NX, NY, 6, 3 * GD)).reshape(NX * NY, 6, 3 * GD)
    mix = lax.all_to_all(mix, ("x", "y"), 0, 0, tiled=True)
    mix = copy_gather(mix.reshape(NX * NY * 6, 3 * GD), ("z", "c"))
    mix = mix.reshape(NZ, NC, NX, NY, 6, 3 * GD).transpose(2, 0, 1, 3, 4, 5)
    tokens4 = ordered(ring_gather(tokens[0], "x"), "x")

    rest = jnp.concatenate([p[0].astype(BF) for p in (out_weight, fc1_weight, fc2_weight)], axis=1)
    rest = jnp.pad(rest, ((0, 2), (0, 0)))[None]
    rest, mix, tokens4 = lax.optimization_barrier((rest, mix, tokens4))
    rest_all = lax.all_gather(rest, everyone, axis=0, tiled=True).reshape(8 * 128, D + 2 * FF)

    w_mix = mix.reshape(D, 3 * GD)

    hidden4 = tokens4.astype(F32)
    normed4 = layer_norm(hidden4, vector[0], vector[1]).astype(BF)
    projected = jnp.dot(normed4, w_mix, preferred_element_type=F32)
    group_bias = lax.dynamic_slice_in_dim(vector[2:4], xi * GD, GD, 1)
    q4 = (projected[:, :GD] + group_bias[0]).astype(BF)
    k4 = projected[:, GD : 2 * GD].astype(BF)
    v4 = (projected[:, 2 * GD :] + group_bias[1]).astype(BF)
    kv4 = jnp.concatenate([k4, v4], axis=1)
    wide4 = lax.dot_general(
        widen, normed4, (((0,), (1,)), ((), ())), preferred_element_type=F32
    ).astype(BF)
    kv_own, kv_other = gather_zc(kv4)
    q4, wide4 = lax.optimization_barrier((q4, wide4))
    att4, exact4, stats4 = attend(tab, q4, kv_own, kv_other)
    attended = lax.all_to_all(att4.reshape(NX, ROWS, GD), "x", 0, 0, tiled=True)
    block_out, gradient, normed_two, branch_low, up_low, active, back_attended, early_rows = (
        feed_forward(attended, tokens[0], cotangent[0], vector, rest_all, widen)
    )
    attended = attended.transpose(1, 0, 2).reshape(ROWS, D)
    down_low = cotangent[0]
    back4 = lax.all_to_all(back_attended, "x", 0, 0, tiled=True).reshape(QROWS, GD)
    packed, stats_all = pack(back4, exact4, stats4, q4)
    x_near = ring_near(packed, "z")

    late = (attended, normed_two, down_low, branch_low, up_low, active)

    def outer(left, right):
        return jnp.einsum("rc,re->ce", left, right, preferred_element_type=F32).astype(BF)

    def half_of(value, which):
        size = value.shape[1] // 2
        return lax.dynamic_slice_in_dim(value, which * size, size, 1)

    mine = list(late[:3]) + [half_of(v, core) for v in late[3:]]
    theirs = list(late[:3]) + [half_of(v, 1 - core) for v in late[3:]]
    got = lax.ppermute(jnp.concatenate(theirs, axis=1), "c", SWAP)
    at, both = 0, []
    for value in mine:
        both.append(jnp.concatenate([value, got[:, at : at + value.shape[1]]], axis=0))
        at = at + value.shape[1]
    both, packed = lax.optimization_barrier((both, packed))
    rest_grad, back_in = lax.optimization_barrier((rest_grads(*both), back4))
    rest_grad = lax.psum_scatter(rest_grad, "x", scatter_dimension=0, tiled=True)

    back_q4 = query_grads(tab, q4, back_in, stats_all, kv_own, kv_other)
    back_q4, x_near = lax.optimization_barrier((back_q4, x_near))
    x_own = ring_gather(packed, "z", x_near)
    x_other = lax.ppermute(x_own, "c", SWAP)
    back_kv4 = key_grads(tab, kv4, x_own, x_other)
    mixed4 = jnp.concatenate([back_q4, back_kv4], axis=1)

    joint = joint_grads(wide4, back_q4, back_kv4, rest_grad).reshape(32, 8, MIX + 7 * (D // 2))
    joint = lax.all_to_all(joint, ("z", "c", "y"), 0, 0, tiled=True)
    back_normed4 = dot_nt(mixed4, w_mix)
    _, shift_back = jax.vjp(
        lambda gain, shift: layer_norm(hidden4, gain, shift), vector[0], vector[1]
    )
    gain_one, shift_one = shift_back(back_normed4)
    pieces = back_normed4.astype(BF)

    def piece_of(device):
        return lax.dynamic_slice_in_dim(pieces, lax.rem(device, NX) * ROWS, ROWS, 0)

    back_normed = lax.dynamic_slice_in_dim(back_normed4, xi * ROWS, ROWS, 0)
    for step in (1, 2, 3):
        moved = lax.ppermute(piece_of(xi + step), "x", [(i, (i + step) % 4) for i in range(4)])
        back_normed = back_normed + moved.astype(F32)

    def column_sum(value):
        return jnp.sum(value.astype(F32), axis=0)

    def at_group(value):
        return lax.dynamic_update_slice_in_dim(jnp.zeros((D,), F32), value, xi * GD, 0)

    late_rows = jnp.stack(
        [
            gain_one,
            shift_one,
            at_group(column_sum(back_q4)),
            at_group(column_sum(back_kv4[:, GD:])),
        ]
    )
    vector_part = jnp.concatenate([late_rows, early_rows], axis=0)
    vector_part = vector_part + lax.ppermute(vector_part, "c", SWAP)
    vector_part = sum_ring(vector_part, "y")
    joint, vector_part = lax.optimization_barrier((joint, vector_part))
    vector_total = sum_ring(sum_ring(vector_part, "z"), "x")[None]

    hidden = tokens[0].astype(F32)
    _, first_back = jax.vjp(lambda h: layer_norm(h, vector[0], vector[1]), hidden)
    input_grad = gradient + first_back(back_normed)[0]

    mix_grad = jnp.sum(joint[:, :, :MIX].astype(F32), axis=0).astype(BF)
    mix_grad = lax.all_to_all(
        mix_grad.reshape(8, NX, MIX // NX).transpose(1, 0, 2), "x", 0, 0, tiled=True
    )[:, :6, : 3 * GD].astype(F32)
    mix_grad = (
        mix_grad.reshape(NX, 6, 3, GD).transpose(1, 2, 0, 3).reshape(1, 6, 3 * D)
    )
    wide_sum = jnp.sum(
        joint[:, :, MIX:].reshape(NZ, NC, NY, 8, 7 * (D // 2)).astype(F32), axis=(0, 2)
    )
    top, fill = wide_sum[:, :6], wide_sum[:, 6:, : 3 * D].reshape(NC, 6, D)

    def joined(*parts):
        return jnp.concatenate([part[j] for j in range(NC) for part in parts], axis=1)[None]

    out_grad = joined(top[:, :, 3 * D :])
    fc1_grad = joined(top[:, :, : 2 * D])
    fc2_grad = joined(top[:, :, 2 * D : 3 * D], fill)

    qkv_new = adamw(qkv_weight, qkv_moment, qkv_second, mix_grad, RATE_MATRIX, DECAY_MATRIX)
    out_new = adamw(
        out_weight, out_moment, out_second, out_grad, RATE_MATRIX, DECAY_MATRIX
    )
    fc1_new = adamw(
        fc1_weight, fc1_moment, fc1_second, fc1_grad, RATE_MATRIX, DECAY_MATRIX
    )
    fc2_new = adamw(
        fc2_weight, fc2_moment, fc2_second, fc2_grad, RATE_MATRIX, DECAY_MATRIX
    )
    vec_new = adamw(vectors, vector_moment, vector_second, vector_total, RATE_VECTOR, 0.0)
    return (
        block_out[None],
        input_grad[None],
        *qkv_new,
        *out_new,
        *fc1_new,
        *fc2_new,
        *vec_new,
    )


def solution(mesh):
    grid = Mesh(mesh.devices.reshape(NX, NZ, NC, NY), ("x", "z", "c", "y"))
    rows = P("y", ("x", "z", "c"), None)
    weight = P(None, ("x", "z", "c", "y"), None)
    in_specs = (rows, rows, P()) + (weight,) * 4 + (P(),) + (weight,) * 8 + (P(), P())
    out_specs = (rows, rows) + (weight,) * 12 + (P(), P(), P())
    return jax.shard_map(local, mesh=grid, in_specs=in_specs, out_specs=out_specs, check_vma=False)
```
